512 devices in a mesh: seq: 16 (over y, core), head: 4 (over x), ivf: 8 (over z).
Axes of the slice: x: 4, y: 8, z: 8, core: 2. Of those that a mesh axis runs over, the one named last changes fastest.
Arguments:
- hidden_in: bfloat16 [8192, 4096], P('seq'), may hold values from -8 to 8
- w_x: bfloat16 [4096, 8192], P('seq', ('head', 'ivf')), may hold values from -0.09375 to 0.09375
- w_z: bfloat16 [4096, 8192], P('seq', ('head', 'ivf')), may hold values from -0.09375 to 0.09375
- w_dt: bfloat16 [4096, 128], P('seq', ('head', 'ivf')), may hold values from -0.09375 to 0.09375
- w_bc: bfloat16 [4096, 2048], P('seq', 'head'), may hold values from -0.0078125 to 0.0078125
- dt_bias: float32 [128], P(('head', 'ivf')), may hold values from -1 to 1
- a_rate: float32 [128], P(('head', 'ivf')), may hold values from 2.4414063e-05 to 0.1
- d_skip: float32 [128], P(('head', 'ivf')), may hold values from 0.5 to 2
- norm_gain: float32 [8192], P(('head', 'ivf')), may hold values from 0.1 to 1.9
- w_out: bfloat16 [8192, 4096], P(('head', 'ivf'), 'seq'), may hold values from -0.0625 to 0.0625
- span_lengths: int32 [32], replicated, may hold values from 1 to 512, 8192 in all
- owners: int32 [32, 1], replicated, may hold values from 0 to 7; in each aligned block of 32 rows (0 to 31, 32 to 63, ...) at most 6 rows name the same one
Outputs:
- ivf_rows: float32 [8, 6, 4096], P('ivf', None, ('seq', 'head'))
The draws below stay inside these ranges and needn't reach their ends.
Inputs may be any that keep to these rules, and one draw needn't show every extreme that they name: `span_lengths`: the spans cover the slab's tokens in order; the longest has exactly 512 tokens. `owners`: no owner has more than 6 spans, and some owner has exactly 6.
All inputs are finite; a program needn't handle non-finite values.
Results may differ from the reference program's by a relative error of at most 0.0045.
Values may be sent and summed in bfloat16 or wider, within the bound.
A program may use at most 64 MiB of HBM per device.

```python
import math
import jax
import jax.numpy as jnp
import numpy as np
from jax import lax

D = 4096
HEADS = 128
HEAD_DIM = 64
STATE = 128
GROUPS = 8
STRETCH = 128
SPAN_MOST = 512
INNER = 8192
SLAB = 8192
SPANS = 32
CAP = 6
N_IVF = 8


def draw_hidden_in(key, part):
    key = jax.random.fold_in(key, 11)
    offset_key, noise_key = jax.random.split(key, 2)
    offsets = jnp.clip(jax.random.normal(offset_key, (1, D), jnp.float32), -4.0, 4.0)
    noise_part = jnp.clip(jax.random.normal(noise_key, (SLAB, D), jnp.float32), -4.0, 4.0)
    values = offsets + noise_part
    return values.astype(jnp.bfloat16)


def levels(stream_key, shape, cuts, low, largest):
    def one(dim, parts):
        steps = jax.random.uniform(jax.random.fold_in(jax.random.fold_in(stream_key, 6), dim), (parts,), jnp.float32, low / len(cuts), largest / len(cuts))
        return jnp.repeat(jnp.exp(steps), shape[dim] // parts).reshape((-1,) + (1,) * (len(shape) - dim - 1))

    factor_of = one(*cuts[0])
    for cut in cuts[1:]:
        factor_of = factor_of * one(*cut)
    return factor_of


def length_profile(amount, total, most, lean):
    portions = [(1 << 20) // math.isqrt(standing ** lean) + 1 for standing in range(2, amount + 1)]
    spare, holding = total - most - (amount - 1), [1] * (amount - 1)
    while spare > 0:
        movable = [i for i in range(amount - 1) if holding[i] < most]
        whole, left = sum([portions[i] for i in movable]), spare
        for i in movable:
            extra = min(most - holding[i], max(1, left * portions[i] // whole), spare)
            holding[i] = holding[i] + extra
            spare = spare - extra
    return np.array([most] + holding)


def ragged_sizes(stream_key, amount, total, most, skew):
    if amount == 2:
        one = jax.random.randint(stream_key, (), max(1, total - most), min(most, total - 1) + 1)
        return jnp.stack([one, total - one])
    sizes = jnp.asarray(length_profile(amount, total, most, skew), jnp.int32)
    twos = (amount - 1) // 2
    giver, taker = sizes[1:1 + 2 * twos:2], sizes[2:2 + 2 * twos:2]
    room = jnp.minimum(giver - 1, most - taker)
    moved = jax.random.randint(jax.random.fold_in(stream_key, 1), (twos,), 0, 1 << 20) % (room + 1)
    sizes = sizes.at[1:1 + 2 * twos:2].set(giver - moved).at[2:2 + 2 * twos:2].set(taker + moved)
    return sizes[jax.random.permutation(jax.random.fold_in(stream_key, 2), amount)]


def deal_out(key, own, number, rows, number_of, top, reach, skew):
    ranking = jax.random.permutation(key, number_of)
    crowded, common = shares(number_of, rows * top, reach, skew, True), shares(number_of, rows * top, reach, skew, False)
    places = jnp.arange(number_of)

    def named(sizes, rotation):
        used = int((sizes > 0).sum())
        fixed = max(1, used // 4)
        moved = fixed + (places - fixed + rotation * (used - fixed)) % max(1, number_of - fixed)
        return jnp.zeros((number_of,), jnp.int32).at[ranking[jnp.where(places < fixed, places, moved)]].set(jnp.asarray(sizes, jnp.int32))

    sizes = jnp.where(number % 4 == 0, named(crowded, number // 4), named(common, number - number // 4 - 1))
    mixed = jax.random.permutation(jax.random.fold_in(own, 3), number_of)
    giver, taker = mixed[0:number_of // 2 * 2:2], mixed[1:number_of // 2 * 2:2]
    margin = jnp.minimum(sizes[giver] - 1, reach - sizes[taker]) // 2
    margin = jnp.where((giver == ranking[0]) | (taker == ranking[0]) | (sizes[taker] == 0), 0, jnp.maximum(margin, 0))
    moved = jax.random.randint(jax.random.fold_in(own, 4), (number_of // 2,), 0, 1 << 20) % (margin + 1)
    sizes = sizes.at[giver].add(-moved).at[taker].add(moved)
    labels = jnp.searchsorted(jnp.cumsum(sizes), jnp.arange(rows * top), side="right").astype(jnp.int32)
    grid = labels.reshape(top, rows).T
    grid = grid[jax.random.permutation(jax.random.fold_in(own, 1), rows)]
    rotation = jax.random.randint(jax.random.fold_in(own, 2), (rows, 1), 0, top)
    return jnp.take_along_axis(grid, (jnp.arange(top)[None, :] + rotation) % top, axis=1)


def shares(amount, total, most, skew, full):
    portions = [(1 << 20) // math.isqrt(grade ** skew) + 1 for grade in range(1, amount + 1)]
    largest = most if full else min(most, max(-(-total // amount), total * portions[0] // sum(portions)))
    least = 1 if total - largest >= amount - 1 else 0
    given, spare = [largest] + [least] * (amount - 1), total - largest - least * (amount - 1)
    while spare > 0:
        free = [i for i in range(1, amount) if given[i] < largest] or [i for i in range(1, amount) if given[i] < most]
        whole, budget = sum([portions[i] for i in free]), spare
        for i in free:
            addition = min(most - given[i], max(1, budget * portions[i] // whole), spare)
            given[i] = given[i] + addition
            spare = spare - addition
    return np.array(given)


def centred(own_key, dims, scale, most, cuts=(), held_as=jnp.bfloat16):
    entries = scale * jax.random.normal(own_key, dims, jnp.float32)
    if cuts:
        entries = entries * levels(own_key, dims, cuts, -0.22, 0.18)
    return jnp.clip(entries, -most, most).astype(held_as)


def setup_inputs(seed: int = 0) -> dict:
    arg_keys = jax.random.split(jax.random.key(seed), 13)
    hidden_in = draw_hidden_in(jax.random.fold_in(arg_keys[12], 71), 0)
    w_x = centred(arg_keys[1], (D, INNER), D ** -0.5, 0.09375, ((0, 16), (1, 32)))
    w_z = centred(arg_keys[2], (D, INNER), D ** -0.5, 0.09375, ((0, 16), (1, 32)))
    w_dt = centred(arg_keys[3], (D, HEADS), D ** -0.5, 0.09375, ((0, 16), (1, 32)))
    w_bc = centred(arg_keys[4], (D, 2 * GROUPS * STATE), (D * STATE) ** -0.5, 0.0078125, ((0, 16), (1, 4)))
    dt_bias = jnp.clip(jax.random.uniform(arg_keys[5], (HEADS,), jnp.float32, -1.0, 1.0) * levels(arg_keys[5], (HEADS,), ((0, 32),), -0.4, 0.0), -1.0, 1.0)
    a_rate = jnp.clip(jnp.exp(math.log(0.1) - 8.317766 * jax.random.uniform(arg_keys[6], (HEADS,), jnp.float32) ** levels(arg_keys[6], (HEADS,), ((0, 32),), -0.2, 0.2)), 2.441406286379788e-05, 0.1)
    d_skip = jnp.clip(0.5 + 1.5 * jax.random.uniform(arg_keys[7], (HEADS,), jnp.float32) ** levels(arg_keys[7], (HEADS,), ((0, 32),), -0.2, 0.2), 0.5, 2.0)
    norm_gain = jnp.clip(1.0 + 0.18 * jax.random.normal(arg_keys[8], (INNER,), jnp.float32), 0.1, 1.9)
    w_out = centred(arg_keys[9], (INNER, D), INNER ** -0.5, 0.0625, ((0, 32), (1, 16)))
    span_lengths = ragged_sizes(arg_keys[10], SPANS, SLAB, SPAN_MOST, 1).astype(jnp.int32)
    owners_keys = jax.random.split(jax.random.fold_in(arg_keys[11], 1), SPANS // SPANS)
    owners_turns = jax.random.permutation(jax.random.fold_in(arg_keys[11], 3), SPANS // SPANS)
    owners = jax.vmap(lambda own, number: deal_out(jax.random.fold_in(arg_keys[11], 2), own, number, SPANS, N_IVF, 1, CAP, 2))(owners_keys, owners_turns).reshape((SPANS, 1))
    return dict(hidden_in=hidden_in, w_x=w_x, w_z=w_z, w_dt=w_dt, w_bc=w_bc, dt_bias=dt_bias, a_rate=a_rate, d_skip=d_skip, norm_gain=norm_gain, w_out=w_out, span_lengths=span_lengths, owners=owners)


HIGHEST = lax.Precision.HIGHEST

def ssd_blocks(inputs, step_size, log_decay, b_mat, c_mat, block_len):
    length, head_count, head_width = inputs.shape
    group_count, state_dim = (b_mat.shape[1], b_mat.shape[2])
    per_group = head_count // group_count
    block_count = length // block_len

    def split_blocks(source):
        return source.reshape((block_count, block_len) + source.shape[1:])
    blocks = tuple((split_blocks(source) for source in (inputs, step_size, log_decay, b_mat, c_mat)))
    lower_tri = jnp.tril(jnp.ones((block_len, block_len), dtype=bool))

    def advance(carried, current):
        block_x, block_dt, block_decay, block_b, block_c = current
        running = jnp.cumsum(block_decay, axis=0)
        head_b = jnp.repeat(block_b, per_group, axis=1)
        head_c = jnp.repeat(block_c, per_group, axis=1)
        scores = jnp.einsum('tgn,sgn->gts', block_c, block_b, precision=HIGHEST)
        scores = jnp.repeat(scores, per_group, axis=0)
        between = running.T[:, :, None] - running.T[:, None, :]
        decays = jnp.where(lower_tri, jnp.exp(jnp.where(lower_tri, between, 0.0)), 0.0)
        weights = scores * decays * block_dt.T[:, None, :]
        within = jnp.einsum('hts,shp->thp', weights, block_x, precision=HIGHEST)
        earlier = jnp.exp(running)[:, :, None] * jnp.einsum('thn,hpn->thp', head_c, carried, precision=HIGHEST)
        final_decay = running[-1]
        tail_weight = jnp.exp(final_decay[None, :] - running) * block_dt
        updated = jnp.exp(final_decay)[:, None, None] * carried + jnp.einsum('th,thp,thn->hpn', tail_weight, block_x, head_b, precision=HIGHEST)
        return (updated, within + earlier)
    start_state = jnp.zeros((head_count, head_width, state_dim), jnp.float32)
    end_state, outputs = lax.scan(advance, start_state, blocks)
    return (outputs.reshape(length, head_count, head_width), end_state)

def span_average(span_lengths, first_pos, token_count):
    span_ends = jnp.cumsum(span_lengths)
    starts = span_ends - span_lengths
    positions = first_pos + jnp.arange(token_count, dtype=jnp.int32)
    inside = (positions[None, :] >= starts[:, None]) & (positions[None, :] < span_ends[:, None])
    return inside.astype(jnp.float32) / span_lengths[:, None].astype(jnp.float32)

def slot_matrix(owner_ids, owner_count, capacity):
    member = (owner_ids[:, None] == jnp.arange(owner_count, dtype=jnp.int32)[None, :]).astype(jnp.int32)
    order_in = lax.optimization_barrier(jnp.sum((jnp.cumsum(member, axis=0) - 1) * member, axis=1))
    slot_ids = owner_ids * capacity + order_in
    return (jnp.arange(owner_count * capacity, dtype=jnp.int32)[:, None] == slot_ids[None, :]).astype(jnp.float32)

def reference(hidden_in, w_x, w_z, w_dt, w_bc, dt_bias, a_rate, d_skip, norm_gain, w_out, span_lengths, owners):
    inner_x = jnp.dot(hidden_in, w_x, preferred_element_type=jnp.float32).astype(jnp.bfloat16)
    gate_z = jnp.dot(hidden_in, w_z, preferred_element_type=jnp.float32).astype(jnp.bfloat16)
    bc_proj = jnp.dot(hidden_in, w_bc, preferred_element_type=jnp.float32).astype(jnp.bfloat16)
    step_size = jax.nn.softplus(jnp.dot(hidden_in, w_dt, preferred_element_type=jnp.float32) + dt_bias)
    log_decay = -step_size * a_rate
    paired = bc_proj.astype(jnp.float32).reshape(SLAB, GROUPS, 2, STATE)
    inputs = inner_x.astype(jnp.float32).reshape(SLAB, HEADS, HEAD_DIM)
    scanned, end_state = ssd_blocks(inputs, step_size, log_decay, paired[:, :, 0], paired[:, :, 1], STRETCH)
    with_skip = scanned + d_skip[None, :, None] * inputs
    gated_y = with_skip * jax.nn.silu(gate_z.astype(jnp.float32)).reshape(SLAB, HEADS, HEAD_DIM)
    mean_sq = lax.optimization_barrier(jnp.sum(gated_y * gated_y, axis=2, keepdims=True)) / HEAD_DIM
    normed = ((gated_y * lax.rsqrt(mean_sq + 1e-05)).reshape(SLAB, INNER) * norm_gain).astype(jnp.bfloat16)
    averaging = span_average(span_lengths, 0, SLAB)
    pooled_y = jnp.dot(averaging, normed.astype(jnp.float32), precision=HIGHEST)
    pooled = jnp.dot(averaging, hidden_in.astype(jnp.float32), precision=HIGHEST) + jnp.dot(pooled_y, w_out.astype(jnp.float32), precision=HIGHEST)
    slot_rows = slot_matrix(owners[:, 0], N_IVF, CAP)
    return jnp.dot(slot_rows, pooled, precision=HIGHEST).reshape(N_IVF, CAP, D)
```

```python
import jax
import jax.numpy as jnp
from jax import lax
from jax.experimental import pallas as pl
from jax.experimental.pallas import tpu as pltpu
from jax.sharding import PartitionSpec as P

HEADS = 128
HEAD_DIM = 64
STATE = 128
GROUPS = 8
CAP = 6

SEQ = 16
RING = SEQ // 2
NHEAD = 4
NIVF = 8
TOK = 512
KB = 256
CH = 256
LH = CH // HEAD_DIM
SHARE = 4
BCR = 2 * STATE // SHARE
DTR = 16
AR = KB + BCR + DTR
T_CUT = (KB, BCR + DTR, 4, 3)
X_CUTS = ((0, 128, 3, 4), (128, 128, 4, 3))
Z_CUTS = ((0, 128, 3, 4), (128, 128, 4, 3))
SPANS = 32
F32 = jnp.float32
BF16 = jnp.bfloat16
HIGHEST = lax.Precision.HIGHEST
MESH = pl.DeviceIdType.MESH

NN = (((1,), (0,)), ((), ()))
NT = (((1,), (1,)), ((), ()))
TN = (((0,), (0,)), ((), ()))


def dot(a, b, dims=NN, precision=None):
    return lax.dot_general(a, b, dims, precision=precision, preferred_element_type=F32)


def iota(shape, dim):
    return lax.broadcasted_iota(jnp.int32, shape, dim)


def split(v):
    high = v.astype(BF16)
    return high, (v - high.astype(F32)).astype(BF16)


def outward(k, middle):
    return middle + (1 - 2 * (k % 2)) * ((k + 1) // 2)


def lane_sums(v):
    width = v.shape[1]
    lane = iota(v.shape, 1)
    step = 1
    while step < width:
        v = v + jnp.where(lane >= step, pltpu.roll(v, step, 1), 0.0)
        step *= 2
    return v


def kernel(
    hid_hbm, wx_hbm, wz_hbm, wdt_hbm, wbc_hbm, wout_hbm, len_ref, own_ref, bias_ref, rate_ref, skip_ref, gain_ref,
    out_ref,
    hid, abuf, zbuf, xacc, zacc, bacc, bcbuf, wbc, wdt, wout, wpad, pick_slots, ins,
    usrc, urecv, smsg, srecv, sout, sin, scores, cumt, dtt, ybuf, ecum,
    psrc, psib, pall, phalf, fsrc, frecv,
    ld_sem, ring_send, ring_recv, sib_send, sib_recv, bc_send, bc_recv,
    a2a_send, a2a_recv, p_send, p_recv, f_send, f_recv,
):
    seq = lax.axis_index("seq")
    head = lax.axis_index("head")
    ivf = lax.axis_index("ivf")
    y = seq // 2
    c = seq % 2
    up = ((y + 1) % RING) * 2 + c
    down = ((y + RING - 1) % RING) * 2 + c
    sibling = y * 2 + 1 - c
    piece = ivf % SHARE

    def other(k):
        return lax.rem(seq + outward(k, SEQ // 2), SEQ)

    def far(k):
        h = lax.rem(head + outward(k // NIVF, NHEAD // 2), NHEAD)
        o = lax.rem(ivf + outward(k % NIVF, NIVF // 2), NIVF)
        return h, o

    n_seq, n_far = SEQ - 1, NHEAD * NIVF - 1

    lanes = pl.ds(pl.multiple_of((ivf // SHARE) * (2 * STATE) + (piece // 2) * 128, 128), 128)
    loads = [
        pltpu.make_async_copy(wbc_hbm.at[:, lanes], wbc, ld_sem.at[0]),
        pltpu.make_async_copy(wdt_hbm, wdt, ld_sem.at[1]),
        pltpu.make_async_copy(wx_hbm, abuf.at[0, pl.ds(0, KB)], ld_sem.at[2]),
        pltpu.make_async_copy(wz_hbm, zbuf.at[0], ld_sem.at[3]),
        pltpu.make_async_copy(hid_hbm, hid, ld_sem.at[4]),
        pltpu.make_async_copy(wout_hbm, wout, ld_sem.at[5]),
    ]
    for load in loads:
        load.start()

    barrier = pltpu.get_barrier_semaphore()

    def greet_far(k, carry):
        h, o = far(k)
        pl.semaphore_signal(barrier, inc=1, device_id={"head": h, "ivf": o}, device_id_type=MESH)
        return carry

    def greet_seq(k, carry):
        pl.semaphore_signal(barrier, inc=1, device_id={"seq": other(k)}, device_id_type=MESH)
        return carry

    lax.fori_loop(0, n_far, greet_far, 0)
    lax.fori_loop(0, n_seq, greet_seq, 0)

    loads[0].wait()
    loads[1].wait()
    row = iota((BCR, 128), 0) + (piece % 2) * BCR
    take = (row == iota((BCR, 128), 1)).astype(F32).astype(BF16)
    abuf[0, KB : KB + BCR, :] = dot(take, wbc[...], NT).astype(BF16)
    take = (iota((DTR, LH), 0) == iota((DTR, LH), 1)).astype(F32).astype(BF16)
    abuf[0, KB + BCR : AR, :] = dot(take, wdt[...]).astype(BF16)
    xacc[...] = jnp.zeros_like(xacc)
    zacc[...] = jnp.zeros_like(zacc)
    bacc[...] = jnp.zeros_like(bacc)
    loads[2].wait()
    pl.semaphore_wait(barrier, n_seq + n_far)

    cuts = (T_CUT,) + X_CUTS + Z_CUTS

    def ring_ref(n, at):
        buf = abuf if n < 3 else zbuf
        return buf.at[at, pl.ds(cuts[n][0], cuts[n][1])]

    def ring_copy(n, direction, d):
        if direction == 0:
            src, dst, peer = d, d + 1, up
        else:
            src, dst, peer = d + 4 * ((d + 3) // 4), d + 5 - 4 * (d // 3), down
        return pltpu.make_async_remote_copy(
            src_ref=ring_ref(n, src),
            dst_ref=ring_ref(n, dst),
            send_sem=ring_send.at[n, direction, d],
            recv_sem=ring_recv.at[n, dst],
            device_id={"seq": peer},
            device_id_type=MESH,
        )

    def ring_wait(n, at):
        ref = ring_ref(n, at)
        pltpu.make_async_copy(ref, ref, ring_recv.at[n, at]).wait()

    def sib_copy(w, at, part=None):
        buf, sem = (abuf, zbuf)[w], 3 * w
        rows = pl.ds(0, (AR, KB)[w])
        if part == 0:
            rows = pl.ds(0, KB)
        if part == 1:
            rows, sem = pl.ds(KB, AR - KB), 1
        return pltpu.make_async_remote_copy(
            src_ref=buf.at[at, rows],
            dst_ref=buf.at[at + 8, rows],
            send_sem=sib_send.at[sem, at],
            recv_sem=sib_recv.at[sem, at],
            device_id={"seq": sibling},
            device_id_type=MESH,
        )

    def k_block(at):
        m = at % 8
        rel = (m // 5) * (2 * m - 4) - m
        side = at // 8
        core = c + side - 2 * c * side
        return ((y + rel + RING) % RING) * 2 + core

    def hid_cols(at):
        return hid[:, pl.ds(pl.multiple_of(k_block(at) * KB, KB), KB)]

    def mul_t(at):
        bacc[...] += dot(abuf[at, KB:AR, :], hid_cols(at), NT)

    def mul_x(at):
        xacc[...] += dot(hid_cols(at), abuf[at, 0:KB, :])

    def mul_z(at):
        zacc[...] += dot(hid_cols(at), zbuf[at])

    def mul_a(at):
        mul_t(at)
        mul_x(at)

    def two(mul, base):
        def one(i, carry):
            mul(base + 4 * i)
            return carry

        lax.fori_loop(0, 2, one, 0)

    for n in (0, 1, 2):
        ring_copy(n, 0, 0).start()
        ring_copy(n, 1, 0).start()
    sib_copy(0, 0).start()

    lengths = jnp.broadcast_to(len_ref[...].astype(F32), (8, SPANS))
    ends = lengths
    step = 1
    while step < SPANS:
        moved = jnp.concatenate([jnp.zeros((8, step), F32), ends[:, : SPANS - step]], axis=1)
        ends = ends + moved
        step *= 2
    starts = ends - lengths
    member = (jnp.broadcast_to(own_ref[...], (8, SPANS)) == iota((8, SPANS), 0)).astype(F32)
    before = (iota((SPANS, SPANS), 0) < iota((SPANS, SPANS), 1)).astype(F32)
    rank = dot(member, before)
    slot = iota((8, SPANS), 0).astype(F32)
    pos = (iota((8, TOK), 1) + seq * TOK).astype(F32)
    own_first = jnp.zeros((8, 1), F32)
    own_last = jnp.zeros((8, 1), F32)
    for o in range(NIVF):
        chosen = jnp.where(rank[o : o + 1, :] == slot, member[o : o + 1, :], 0.0)
        pick_slots[o * 8 : o * 8 + 8, :] = chosen
        first = jnp.sum(chosen * starts, axis=1, keepdims=True)
        last = jnp.sum(chosen * ends, axis=1, keepdims=True)
        own_first = jnp.where(ivf == o, first, own_first)
        own_last = jnp.where(ivf == o, last, own_last)
    own_ins = ((pos >= own_first) & (pos < own_last)).astype(F32).astype(BF16)
    own_inv = 1.0 / jnp.maximum(own_last - own_first, 1.0)
    span_row = iota((SPANS, SPANS), 0) == iota((SPANS, SPANS), 1)
    span_first = jnp.sum(jnp.where(span_row, starts[0:1, :], 0.0), axis=1, keepdims=True)
    span_last = jnp.sum(jnp.where(span_row, ends[0:1, :], 0.0), axis=1, keepdims=True)
    span_pos = (iota((SPANS, TOK), 1) + seq * TOK).astype(F32)
    ins[...] = ((span_pos >= span_first) & (span_pos < span_last)).astype(F32)
    span_inv = 1.0 / (span_last - span_first)

    loads[4].wait()

    def u_block(s, carry):
        cols = pl.ds(pl.multiple_of(s * KB + (head // 2) * 128, 128), 128)
        usrc[s] = dot(own_ins, hid[:, cols]) * own_inv
        return carry

    lax.fori_loop(0, SEQ, u_block, 0)

    def a2a_start(kind, src_of, dst_of):
        def one(k, carry):
            pltpu.make_async_remote_copy(
                src_ref=src_of(k),
                dst_ref=dst_of(k),
                send_sem=a2a_send.at[kind],
                recv_sem=a2a_recv.at[kind],
                device_id={"seq": other(k)},
                device_id_type=MESH,
            ).start()
            return carry

        lax.fori_loop(0, n_seq, one, 0)

    def a2a_wait(kind, ref):
        pltpu.make_async_copy(ref, ref, a2a_recv.at[kind]).wait()

    def a2a_sent(kind, ref):
        pltpu.make_async_copy(ref, ref, a2a_send.at[kind]).wait()

    a2a_start(0, lambda k: usrc.at[other(k)], lambda k: urecv.at[k])

    mul_a(0)
    sib_copy(0, 0).wait_recv()
    mul_a(8)
    loads[3].wait()

    def a_step(d, carry):
        ring_wait(0, d)
        ring_copy(0, 0, d).start()
        ring_wait(0, 4 + d)

        @pl.when(d < 3)
        def _():
            ring_copy(0, 1, d).start()

        @pl.when(d == 3)
        def _():
            ring_copy(3, 1, 0).start()

        ring_wait(1, 4 + d)
        ring_copy(1, 1, d).start()
        ring_wait(1, d)

        @pl.when(d < 3)
        def _():
            ring_copy(1, 0, d).start()

        @pl.when(d == 3)
        def _():
            ring_copy(4, 0, 0).start()

        ring_wait(2, d)
        ring_copy(2, 0, d).start()
        sib_copy(0, d).start()
        ring_wait(2, 4 + d)

        @pl.when(d < 3)
        def _():
            ring_copy(2, 1, d).start()

        @pl.when(d == 3)
        def _():
            ring_copy(4, 1, 0).start()

        sib_copy(0, 4 + d).start()
        two(mul_a, d)
        sib_copy(0, d).wait_recv()
        sib_copy(0, 4 + d).wait_recv()
        two(mul_a, 8 + d)
        return carry

    lax.fori_loop(1, 4, a_step, 0)
    ring_wait(0, 4)
    sib_copy(0, 4, 1).start()
    ring_copy(3, 0, 0).start()
    sib_copy(1, 0).start()
    mul_t(4)
    sib_copy(0, 4, 1).wait_recv()
    mul_t(12)

    bcbuf[piece] = bacc[0:BCR, :].astype(BF16)

    def bc_copy(j):
        peer = (ivf // SHARE) * SHARE + lax.rem(piece + j, SHARE)
        return pltpu.make_async_remote_copy(
            src_ref=bcbuf.at[piece],
            dst_ref=bcbuf.at[piece],
            send_sem=bc_send,
            recv_sem=bc_recv,
            device_id={"ivf": peer},
            device_id_type=MESH,
        )

    for j in range(1, SHARE):
        bc_copy(j).start()
    ring_wait(1, 4)
    ring_wait(2, 4)
    sib_copy(0, 4, 0).start()
    mul_x(4)

    diag = iota((8, LH), 0) == iota((8, LH), 1)
    bias = jnp.sum(jnp.where(diag, bias_ref[...], 0.0), axis=1, keepdims=True)
    rate = jnp.sum(jnp.where(diag, rate_ref[...], 0.0), axis=1, keepdims=True)
    skip = jnp.sum(jnp.where(diag, skip_ref[...], 0.0), axis=1, keepdims=True)
    raw = bacc[BCR : BCR + 8, :] + bias
    step_size = jnp.maximum(raw, 0.0) + jnp.log1p(jnp.exp(-jnp.abs(raw)))
    cum = lane_sums(-step_size * rate)
    total = cum[:, TOK - 1 : TOK]
    cumt[...] = cum
    dtt[...] = step_size
    spread = (iota((8, CH), 1) // HEAD_DIM == iota((8, CH), 0)).astype(F32)
    tail = dot(jnp.exp(total - cum) * step_size, spread, TN, HIGHEST)
    ecum[...] = dot(jnp.exp(cum), spread, TN, HIGHEST)
    total_row = jnp.sum(total * spread, axis=0, keepdims=True)
    skip_row = jnp.sum(skip * spread, axis=0, keepdims=True)
    sib_copy(0, 4, 0).wait_recv()
    mul_x(12)
    x_b = xacc[...].astype(BF16)
    x_f = x_b.astype(F32)
    w_hi, w_lo = split(x_f * tail)

    pltpu.make_async_copy(bcbuf.at[pl.ds(0, SHARE - 1)], bcbuf.at[pl.ds(0, SHARE - 1)], bc_recv).wait()
    b_t = jnp.concatenate([bcbuf[0], bcbuf[1]], axis=0)
    end_state = (dot(b_t, w_hi) + dot(b_t, w_lo)).astype(BF16)
    d_hi = total_row.astype(BF16)
    left = total_row - d_hi.astype(F32)
    d_mid = left.astype(BF16)
    d_lo = (left - d_mid.astype(F32)).astype(BF16)
    sub16 = iota((16, CH), 0)
    decay_rows = jnp.where(
        sub16 == 0,
        d_hi.astype(F32),
        jnp.where(sub16 == 1, d_mid.astype(F32), jnp.where(sub16 == 2, d_lo.astype(F32), 0.0)),
    ).astype(BF16)
    for s in range(SEQ):
        r, half = s // 2, s % 2
        cols = slice(half * 128, half * 128 + 128)
        smsg[s, 0:16, :] = end_state[r * 16 : r * 16 + 16, cols]
        smsg[s, 16:32, :] = decay_rows[:, cols]
    a2a_start(1, lambda k: smsg.at[other(k)], lambda k: srecv.at[seq])
    srecv[seq] = smsg[seq]

    def z_step(d):
        ring_wait(4, d)
        ring_copy(4, 0, d).start()
        ring_wait(3, 4 + d)
        ring_copy(3, 1, d).start()
        ring_wait(3, d)
        if d < 3:
            ring_copy(3, 0, d).start()
        sib_copy(1, d).start()
        ring_wait(4, 4 + d)
        if d < 3:
            ring_copy(4, 1, d).start()
        sib_copy(1, 4 + d).start()

    def z_use(d):
        two(mul_z, d)
        sib_copy(1, d).wait_recv()
        sib_copy(1, 4 + d).wait_recv()
        two(mul_z, 8 + d)

    z_step(1)
    mul_z(0)
    sib_copy(1, 0).wait_recv()
    mul_z(8)
    c_t = jnp.concatenate([bcbuf[2], bcbuf[3]], axis=0)
    c_m = c_t.astype(F32).T.astype(BF16)
    scores[...] = dot(c_m, b_t)
    ybuf[...] = x_f * skip_row
    z_use(1)

    def one_head(h, carry):
        pick = (iota((8, 128), 0) == h).astype(F32)
        rep = dot(cumt[...], pick, TN, HIGHEST)
        xm = jnp.where(iota((TOK, CH), 1) // HEAD_DIM == h, x_f, 0.0).astype(BF16)
        cum_row = cumt[pl.ds(h, 1), :]
        dt_row = dtt[pl.ds(h, 1), :]
        for i in range(4):
            highs, lows = [], []
            here = slice(i * 128, i * 128 + 128)
            for k in range(i + 1):
                cols = slice(k * 128, k * 128 + 128)
                between = rep[here, :] - cum_row[:, cols]
                if k == i:
                    between = jnp.where(iota((128, 128), 0) >= iota((128, 128), 1), between, -1e30)
                weight = scores[here, cols] * jnp.exp(between) * dt_row[:, cols]
                high, low = split(weight)
                highs.append(high)
                lows.append(low)
            if i:
                highs, lows = [jnp.concatenate(highs, axis=1)], [jnp.concatenate(lows, axis=1)]
            rows = xm[0 : i * 128 + 128, :]
            ybuf[here, :] += dot(highs[0], rows) + dot(lows[0], rows)
        return carry

    lax.fori_loop(0, 2, one_head, 0)
    z_step(2)
    a2a_wait(1, srecv.at[pl.ds(0, n_seq)])

    def enter(s, carried):
        sout[s] = carried.astype(BF16)
        block = srecv[s].astype(F32)
        decay = jnp.exp(block[16:17, :] + block[17:18, :] + block[18:19, :])
        return decay * carried + block[0:16, :]

    lax.fori_loop(0, SEQ, enter, jnp.zeros((16, 128), F32))
    a2a_start(2, lambda k: sout.at[other(k)], lambda k: sin.at[seq])
    sin[seq] = sout[seq]
    z_use(2)
    lax.fori_loop(2, 4, one_head, 0)

    z_step(3)
    z_use(3)
    loads[5].wait()
    at_col = iota((CH, NHEAD * 128), 1)
    wanted = (at_col // 128) * 64 + at_col % 128
    take = (at_col % 128 < 64) & (wanted == iota((CH, NHEAD * 128), 0))
    wpad[...] = dot(wout[...], take.astype(F32).astype(BF16)).astype(BF16)
    ring_wait(3, 4)
    ring_wait(4, 4)
    sib_copy(1, 4).start()
    mul_z(4)
    sib_copy(1, 4).wait_recv()
    mul_z(12)
    z = zacc[...].astype(BF16).astype(F32)
    gate = z / (1.0 + jnp.exp(-z))

    a2a_wait(2, sin.at[pl.ds(0, n_seq)])
    entering = jnp.concatenate(
        [jnp.concatenate([sin[2 * r], sin[2 * r + 1]], axis=1) for r in range(8)], axis=0
    )
    gated = (ybuf[...] + ecum[...] * dot(c_m, entering)) * gate
    sq_hi, sq_lo = split(gated * gated)
    same = (iota((CH, CH), 0) // HEAD_DIM == iota((CH, CH), 1) // HEAD_DIM).astype(F32).astype(BF16)
    mean_sq = (dot(sq_hi, same) + dot(sq_lo, same)) * (1.0 / HEAD_DIM)
    normed = (gated * lax.rsqrt(mean_sq + 1e-05) * gain_ref[...]).astype(BF16)
    pooled = dot(ins[...].astype(BF16), normed) * span_inv
    psrc[0] = pooled[:, 0:128]
    psrc[1] = pooled[:, 128:256]

    def to_sibling(kind, src, dst):
        return pltpu.make_async_remote_copy(
            src_ref=src,
            dst_ref=dst,
            send_sem=p_send.at[kind],
            recv_sem=p_recv.at[kind],
            device_id={"seq": sibling},
            device_id_type=MESH,
        )

    first_half = to_sibling(0, psrc.at[1 - c], psib)
    first_half.start()
    first_half.wait_recv()
    pall[y] = psrc[c] + psib[...]

    def p_start(k, carry):
        peer = lax.rem(y + outward(k, RING // 2), RING) * 2 + c
        pltpu.make_async_remote_copy(
            src_ref=pall.at[y],
            dst_ref=pall.at[y],
            send_sem=p_send.at[1],
            recv_sem=p_recv.at[1],
            device_id={"seq": peer},
            device_id_type=MESH,
        ).start()
        return carry

    lax.fori_loop(0, RING - 1, p_start, 0)
    most = pall.at[pl.ds(0, RING - 1)]
    pltpu.make_async_copy(most, most, p_recv.at[1]).wait()
    phalf[c] = jnp.sum(pall[...], axis=0)
    second_half = to_sibling(2, phalf.at[c], phalf.at[c])
    second_half.start()
    second_half.wait_recv()
    s_hi, s_lo = split(jnp.concatenate([phalf[0], phalf[1]], axis=1))
    slots = pick_slots[...].astype(BF16)
    value = dot(dot(slots, s_hi).astype(BF16), wpad[...]) + dot(
        dot(slots, s_lo).astype(BF16), wpad[...]
    )
    for o in range(NIVF):
        for h in range(NHEAD):
            fsrc[h * NIVF + o] = value[o * 8 : o * 8 + 8, h * 128 : h * 128 + 128]

    def f_start(k, carry):
        h, o = far(k)
        pltpu.make_async_remote_copy(
            src_ref=fsrc.at[h * NIVF + o],
            dst_ref=frecv.at[k],
            send_sem=f_send,
            recv_sem=f_recv,
            device_id={"head": h, "ivf": o},
            device_id_type=MESH,
        ).start()
        return carry

    lax.fori_loop(0, n_far, f_start, 0)

    def sent(d, carry):
        for n in range(5):
            for direction in (0, 1):
                if cuts[n][2 + direction] == 4:
                    ring_copy(n, direction, d).wait_send()
                else:

                    @pl.when(d < 3)
                    def _():
                        ring_copy(n, direction, d).wait_send()

        return carry

    def sib_sent(at, carry):
        @pl.when(at != 4)
        def _():
            sib_copy(0, at).wait_send()

        sib_copy(1, at).wait_send()
        return carry

    lax.fori_loop(0, 4, sent, 0)
    lax.fori_loop(0, 8, sib_sent, 0)
    sib_copy(0, 4, 0).wait_send()
    sib_copy(0, 4, 1).wait_send()
    pltpu.make_async_copy(bcbuf.at[pl.ds(0, SHARE - 1)], bcbuf.at[pl.ds(0, SHARE - 1)], bc_send).wait()
    a2a_sent(0, urecv)
    a2a_sent(1, srecv.at[pl.ds(0, n_seq)])
    a2a_sent(2, sin.at[pl.ds(0, n_seq)])
    first_half.wait_send()
    second_half.wait_send()
    pltpu.make_async_copy(most, most, p_send.at[1]).wait()

    a2a_wait(0, urecv)
    mean_u = usrc[seq] + jnp.sum(urecv[...], axis=0)
    mean_u = jnp.where(head % 2 == 0, mean_u[:, 0:64], mean_u[:, 64:128])
    own = fsrc[head * NIVF + ivf]
    pltpu.make_async_copy(frecv, frecv, f_recv).wait()
    result = (own + jnp.sum(frecv[...], axis=0))[:, 0:64] + mean_u
    out_ref[0] = result[0:CAP, :]
    pltpu.make_async_copy(frecv, frecv, f_send).wait()


def local(
    hidden_in, w_x, w_z, w_dt, w_bc, dt_bias, a_rate, d_skip, norm_gain, w_out, span_lengths, owners
):
    any_spec = pl.BlockSpec(memory_space=pl.ANY)
    vmem_spec = pl.BlockSpec(memory_space=pltpu.VMEM)
    vmem = pltpu.VMEM
    dma = pltpu.SemaphoreType.DMA
    return pl.pallas_call(
        kernel,
        out_shape=jax.ShapeDtypeStruct((1, CAP, 64), F32),
        in_specs=[any_spec] * 6 + [vmem_spec] * 6,
        out_specs=vmem_spec,
        scratch_shapes=[
            vmem((TOK, SEQ * KB), BF16),
            vmem((SEQ, AR, CH), BF16),
            vmem((SEQ, KB, CH), BF16),
            vmem((TOK, CH), F32),
            vmem((TOK, CH), F32),
            vmem((BCR + DTR, TOK), F32),
            vmem((SHARE, BCR, TOK), BF16),
            vmem((KB, 128), BF16),
            vmem((LH, KB), BF16),
            vmem((CH, 256), BF16),
            vmem((CH, NHEAD * 128), BF16),
            vmem((64, SPANS), F32),
            vmem((SPANS, TOK), F32),
            vmem((SEQ, 8, 128), F32),
            vmem((SEQ - 1, 8, 128), F32),
            vmem((SEQ, 32, 128), BF16),
            vmem((SEQ, 32, 128), BF16),
            vmem((SEQ, 16, 128), BF16),
            vmem((SEQ, 16, 128), BF16),
            vmem((TOK, TOK), F32),
            vmem((8, TOK), F32),
            vmem((8, TOK), F32),
            vmem((TOK, CH), F32),
            vmem((TOK, CH), F32),
            vmem((2, SPANS, 128), F32),
            vmem((SPANS, 128), F32),
            vmem((RING, SPANS, 128), F32),
            vmem((2, SPANS, 128), F32),
            vmem((NHEAD * NIVF, 8, 128), F32),
            vmem((NHEAD * NIVF - 1, 8, 128), F32),
            dma((6,)),
            dma((5, 2, 4)),
            dma((5, 8)),
            dma((4, 8)),
            dma((4, 8)),
            dma,
            dma,
            dma((3,)),
            dma((3,)),
            dma((3,)),
            dma((3,)),
            dma,
            dma,
        ],
        compiler_params=pltpu.CompilerParams(
            collective_id=0, has_side_effects=True, vmem_limit_bytes=64 * 1024 * 1024
        ),
    )(
        hidden_in,
        w_x,
        w_z,
        w_dt.T,
        w_bc,
        w_out,
        span_lengths.reshape(1, SPANS),
        owners.T,
        dt_bias.reshape(1, LH),
        a_rate.reshape(1, LH),
        d_skip.reshape(1, LH),
        norm_gain.reshape(1, CH),
    )


def solution(mesh):
    return jax.shard_map(
        local,
        mesh=mesh,
        in_specs=(
            P("seq", None),
            P("seq", ("head", "ivf")),
            P("seq", ("head", "ivf")),
            P("seq", ("head", "ivf")),
            P("seq", "head"),
            P(("head", "ivf")),
            P(("head", "ivf")),
            P(("head", "ivf")),
            P(("head", "ivf")),
            P(("head", "ivf"), "seq"),
            P(),
            P(),
        ),
        out_specs=P("ivf", None, ("seq", "head")),
        check_vma=False,
    )
```

```python
import jax
import jax.numpy as jnp
from jax import lax
from jax.experimental import pallas as pl
from jax.experimental.pallas import tpu as pltpu
from jax.sharding import PartitionSpec as P

HEADS = 128
HEAD_DIM = 64
STATE = 128
GROUPS = 8
CAP = 6

SEQ = 16
RING = SEQ // 2
NHEAD = 4
NIVF = 8
TOK = 512
KB = 256
CH = 256
LH = CH // HEAD_DIM
SHARE = 4
BCR = 2 * STATE // SHARE
HALF = BCR // 2
DTR = 16
AR = KB + BCR + DTR
T_CUT = (KB, BCR + DTR, 4, 3)
X_CUTS = ((0, 128, 3, 4), (128, 128, 4, 3))
Z_CUTS = ((0, 128, 3, 4), (128, 128, 4, 3))
SPANS = 32
F32 = jnp.float32
BF16 = jnp.bfloat16
HIGHEST = lax.Precision.HIGHEST
MESH = pl.DeviceIdType.MESH

NN = (((1,), (0,)), ((), ()))
NT = (((1,), (1,)), ((), ()))
TN = (((0,), (0,)), ((), ()))


def dot(a, b, dims=NN, precision=None):
    return lax.dot_general(a, b, dims, precision=precision, preferred_element_type=F32)


def iota(shape, dim):
    return lax.broadcasted_iota(jnp.int32, shape, dim)


def split(v):
    high = v.astype(BF16)
    return high, (v - high.astype(F32)).astype(BF16)


def outward(k, middle):
    return middle + (1 - 2 * (k % 2)) * ((k + 1) // 2)


def lane_sums(v):
    width = v.shape[1]
    lane = iota(v.shape, 1)
    step = 1
    while step < width:
        v = v + jnp.where(lane >= step, pltpu.roll(v, step, 1), 0.0)
        step *= 2
    return v


def kernel(
    hid_hbm, wx_hbm, wz_hbm, wdt_hbm, wbc_hbm, wout_hbm,
    len_hbm, own_hbm, bias_hbm, rate_hbm, skip_hbm, gain_hbm,
    out_ref,
    len_ref, own_ref, bias_ref, rate_ref, skip_ref, gain_ref,
    hid, abuf, zbuf, xacc, zacc, bacc, bcbuf, wbc, wdt, wout, wpad, pick_slots, ins,
    usrc, urecv, dmsg, drecv, smsg, srecv, sout, sin, scores, cumt, dtt, ybuf, ecum,
    psrc, psib, pall, phalf, fsrc, frecv,
    ld_sem, ring_send, ring_recv, sib_send, sib_recv, bc_send, bc_recv,
    a2a_send, a2a_recv, p_send, p_recv, f_send, f_recv,
):
    seq = lax.axis_index("seq")
    head = lax.axis_index("head")
    ivf = lax.axis_index("ivf")
    y = seq // 2
    c = seq % 2
    up = ((y + 1) % RING) * 2 + c
    down = ((y + RING - 1) % RING) * 2 + c
    sibling = y * 2 + 1 - c
    piece = ivf % SHARE

    def other(k):
        return lax.rem(seq + outward(k, SEQ // 2), SEQ)

    def far(k):
        h = lax.rem(head + outward(k // NIVF, NHEAD // 2), NHEAD)
        o = lax.rem(ivf + outward(k % NIVF, NIVF // 2), NIVF)
        return h, o

    n_seq, n_far = SEQ - 1, NHEAD * NIVF - 1

    lanes = pl.ds(pl.multiple_of((ivf // SHARE) * (2 * STATE), 2 * STATE), 2 * STATE)
    loads = [
        pltpu.make_async_copy(wbc_hbm.at[:, lanes], wbc, ld_sem.at[0]),
        pltpu.make_async_copy(wdt_hbm, wdt, ld_sem.at[1]),
        pltpu.make_async_copy(wx_hbm, abuf.at[0, pl.ds(0, KB)], ld_sem.at[2]),
        pltpu.make_async_copy(wz_hbm, zbuf.at[0], ld_sem.at[3]),
        pltpu.make_async_copy(hid_hbm, hid, ld_sem.at[4]),
        pltpu.make_async_copy(wout_hbm, wout, ld_sem.at[5]),
        pltpu.make_async_copy(len_hbm, len_ref, ld_sem.at[6]),
        pltpu.make_async_copy(own_hbm, own_ref, ld_sem.at[7]),
        pltpu.make_async_copy(bias_hbm, bias_ref, ld_sem.at[8]),
        pltpu.make_async_copy(rate_hbm, rate_ref, ld_sem.at[9]),
        pltpu.make_async_copy(skip_hbm, skip_ref, ld_sem.at[10]),
        pltpu.make_async_copy(gain_hbm, gain_ref, ld_sem.at[11]),
    ]
    barrier = pltpu.get_barrier_semaphore()

    def greet_far(k, carry):
        h, o = far(k)
        pl.semaphore_signal(barrier, inc=1, device_id={"head": h, "ivf": o}, device_id_type=MESH)
        return carry

    def greet_seq(k, carry):
        pl.semaphore_signal(barrier, inc=1, device_id={"seq": other(k)}, device_id_type=MESH)
        return carry

    lax.fori_loop(0, n_far, greet_far, 0)
    lax.fori_loop(0, n_seq, greet_seq, 0)
    for load in loads:
        load.start()

    loads[0].wait()
    loads[1].wait()
    row = iota((BCR, 2 * STATE), 0)
    row = row + (row // HALF) * (STATE - HALF) + piece * HALF
    take = (row == iota((BCR, 2 * STATE), 1)).astype(F32).astype(BF16)
    abuf[0, KB : KB + BCR, :] = dot(take, wbc[...], NT).astype(BF16)
    take = (iota((DTR, LH), 0) == iota((DTR, LH), 1)).astype(F32).astype(BF16)
    abuf[0, KB + BCR : AR, :] = dot(take, wdt[...]).astype(BF16)
    loads[2].wait()
    pl.semaphore_wait(barrier, n_seq + n_far)

    cuts = (T_CUT,) + X_CUTS + Z_CUTS

    def ring_ref(n, at):
        buf = abuf if n < 3 else zbuf
        return buf.at[at, pl.ds(cuts[n][0], cuts[n][1])]

    def ring_copy(n, direction, d):
        if direction == 0:
            src, dst, peer = d, d + 1, up
        else:
            src, dst, peer = d + 4 * ((d + 3) // 4), d + 5 - 4 * (d // 3), down
        return pltpu.make_async_remote_copy(
            src_ref=ring_ref(n, src),
            dst_ref=ring_ref(n, dst),
            send_sem=ring_send.at[n, direction, d],
            recv_sem=ring_recv.at[n, dst],
            device_id={"seq": peer},
            device_id_type=MESH,
        )

    def ring_wait(n, at):
        ref = ring_ref(n, at)
        pltpu.make_async_copy(ref, ref, ring_recv.at[n, at]).wait()

    def sib_copy(kind, at):
        buf = (abuf, abuf, zbuf)[kind]
        rows = (pl.ds(0, KB), pl.ds(KB, AR - KB), pl.ds(0, KB))[kind]
        return pltpu.make_async_remote_copy(
            src_ref=buf.at[at, rows],
            dst_ref=buf.at[at + 8, rows],
            send_sem=sib_send.at[kind, at],
            recv_sem=sib_recv.at[kind, at],
            device_id={"seq": sibling},
            device_id_type=MESH,
        )

    def k_block(at):
        m = at % 8
        rel = (m // 5) * (2 * m - 4) - m
        side = at // 8
        core = c + side - 2 * c * side
        return ((y + rel + RING) % RING) * 2 + core

    def hid_cols(at):
        return hid[:, pl.ds(pl.multiple_of(k_block(at) * KB, KB), KB)]

    def mul_t(at):
        bacc[...] += dot(abuf[at, KB:AR, :], hid_cols(at), NT)

    def mul_x(at):
        xacc[...] += dot(hid_cols(at), abuf[at, 0:KB, :])

    def mul_z(at):
        zacc[...] += dot(hid_cols(at), zbuf[at])

    muls = (mul_x, mul_t, mul_z)

    def use_mine(kind, d, count):
        def one(i, carry):
            muls[kind](d + 4 * i)
            return carry

        lax.fori_loop(0, count, one, 0)

    def use_sib(kind, d, count):
        def one(i, carry):
            sib_copy(kind, d + 4 * i).wait_recv()
            muls[kind](8 + d + 4 * i)
            return carry

        lax.fori_loop(0, count, one, 0)

    for n in (0, 1, 2):
        ring_copy(n, 0, 0).start()
        ring_copy(n, 1, 0).start()
    sib_copy(1, 0).start()
    sib_copy(0, 0).start()
    xacc[...] = jnp.zeros_like(xacc)
    zacc[...] = jnp.zeros_like(zacc)
    bacc[...] = jnp.zeros_like(bacc)

    for load in loads[6:]:
        load.wait()
    lengths = jnp.broadcast_to(len_ref[...].astype(F32), (8, SPANS))
    ends = lengths
    step = 1
    while step < SPANS:
        moved = jnp.concatenate([jnp.zeros((8, step), F32), ends[:, : SPANS - step]], axis=1)
        ends = ends + moved
        step *= 2
    starts = ends - lengths
    member = (jnp.broadcast_to(own_ref[...], (8, SPANS)) == iota((8, SPANS), 0)).astype(F32)
    before = (iota((SPANS, SPANS), 0) < iota((SPANS, SPANS), 1)).astype(F32)
    rank = dot(member, before)
    slot = iota((8, SPANS), 0).astype(F32)
    pos = (iota((8, TOK), 1) + seq * TOK).astype(F32)
    own_first = jnp.zeros((8, 1), F32)
    own_last = jnp.zeros((8, 1), F32)
    for o in range(NIVF):
        chosen = jnp.where(rank[o : o + 1, :] == slot, member[o : o + 1, :], 0.0)
        pick_slots[o * 8 : o * 8 + 8, :] = chosen
        first = jnp.sum(chosen * starts, axis=1, keepdims=True)
        last = jnp.sum(chosen * ends, axis=1, keepdims=True)
        own_first = jnp.where(ivf == o, first, own_first)
        own_last = jnp.where(ivf == o, last, own_last)
    own_ins = ((pos >= own_first) & (pos < own_last)).astype(F32).astype(BF16)
    own_inv = 1.0 / jnp.maximum(own_last - own_first, 1.0)
    span_row = iota((SPANS, SPANS), 0) == iota((SPANS, SPANS), 1)
    span_first = jnp.sum(jnp.where(span_row, starts[0:1, :], 0.0), axis=1, keepdims=True)
    span_last = jnp.sum(jnp.where(span_row, ends[0:1, :], 0.0), axis=1, keepdims=True)
    span_pos = (iota((SPANS, TOK), 1) + seq * TOK).astype(F32)
    ins[...] = ((span_pos >= span_first) & (span_pos < span_last)).astype(F32)
    span_inv = 1.0 / (span_last - span_first)

    def a2a_start(kind, src_of, dst_of):
        for k in range(n_seq):
            pltpu.make_async_remote_copy(
                src_ref=src_of(k),
                dst_ref=dst_of(k),
                send_sem=a2a_send.at[kind],
                recv_sem=a2a_recv.at[kind],
                device_id={"seq": other(k)},
                device_id_type=MESH,
            ).start()

    def a2a_wait(kind, ref):
        pltpu.make_async_copy(ref, ref, a2a_recv.at[kind]).wait()

    def a2a_sent(kind, ref):
        pltpu.make_async_copy(ref, ref, a2a_send.at[kind]).wait()

    loads[3].wait()
    loads[4].wait()
    def u_block(s, carry):
        cols = pl.ds(pl.multiple_of(s * KB + (head // 2) * 128, 128), 128)
        usrc[s] = dot(own_ins, hid[:, cols]) * own_inv
        return carry

    lax.fori_loop(0, SEQ, u_block, 0)


    def z_start(n):
        ring_copy(n, 0, 0).start()
        ring_copy(n, 1, 0).start()

    def z_step(n, d):
        ring_wait(n, d)
        if d < cuts[n][2]:
            ring_copy(n, 0, d).start()
        ring_wait(n, 4 + d)
        if d < cuts[n][3]:
            ring_copy(n, 1, d).start()
        if n == 4:
            sib_copy(2, d).start()
            sib_copy(2, 4 + d).start()

    def a_step(d, carry):
        before = 1 + (d + 1) // 3
        ring_wait(0, d)
        ring_copy(0, 0, d).start()
        ring_wait(0, 4 + d)

        @pl.when(d < 3)
        def _():
            ring_copy(0, 1, d).start()

        sib_copy(1, d).start()
        sib_copy(1, 4 + d).start()
        use_mine(1, d - 1, before)
        use_mine(0, d - 1, before)
        ring_wait(1, 4 + d)
        ring_copy(1, 1, d).start()
        ring_wait(1, d)

        @pl.when(d < 3)
        def _():
            ring_copy(1, 0, d).start()

        use_sib(1, d - 1, before)
        use_sib(0, d - 1, before)
        ring_wait(2, d)
        ring_copy(2, 0, d).start()
        ring_wait(2, 4 + d)

        @pl.when(d < 3)
        def _():
            ring_copy(2, 1, d).start()

        sib_copy(0, d).start()
        sib_copy(0, 4 + d).start()

        @pl.when(d == 2)
        def _():
            z_start(3)
            z_start(4)

        @pl.when(d == 3)
        def _():
            z_step(3, 1)
            z_step(4, 1)

        return carry

    lax.fori_loop(1, 4, a_step, 0)
    ring_wait(0, 4)
    sib_copy(1, 4).start()
    use_mine(1, 3, 2)
    use_sib(1, 3, 2)
    mul_t(4)
    use_sib(1, 4, 1)

    for part in (0, 1):
        bcbuf[part, piece] = bacc[part * HALF : part * HALF + HALF, :].astype(BF16)

    def bc_copy(part, j):
        peer = (ivf // SHARE) * SHARE + lax.rem(piece + j, SHARE)
        return pltpu.make_async_remote_copy(
            src_ref=bcbuf.at[part, piece],
            dst_ref=bcbuf.at[part, piece],
            send_sem=bc_send.at[part],
            recv_sem=bc_recv.at[part],
            device_id={"ivf": peer},
            device_id_type=MESH,
        )

    def bc_wait(part, sem):
        ref = bcbuf.at[part, pl.ds(0, SHARE - 1)]
        pltpu.make_async_copy(ref, ref, sem.at[part]).wait()

    for j in (2, 1, 3):
        bc_copy(0, j).start()

    diag = iota((8, LH), 0) == iota((8, LH), 1)
    bias = jnp.sum(jnp.where(diag, bias_ref[...], 0.0), axis=1, keepdims=True)
    rate = jnp.sum(jnp.where(diag, rate_ref[...], 0.0), axis=1, keepdims=True)
    skip = jnp.sum(jnp.where(diag, skip_ref[...], 0.0), axis=1, keepdims=True)
    raw = bacc[BCR : BCR + 8, :] + bias
    step_size = jnp.maximum(raw, 0.0) + jnp.log1p(jnp.exp(-jnp.abs(raw)))
    cum = lane_sums(-step_size * rate)
    total = cum[:, TOK - 1 : TOK]
    cumt[...] = cum
    dtt[...] = step_size
    spread = (iota((8, CH), 1) // HEAD_DIM == iota((8, CH), 0)).astype(F32)
    tail = dot(jnp.exp(total - cum) * step_size, spread, TN, HIGHEST)
    ecum[...] = dot(jnp.exp(cum), spread, TN, HIGHEST)
    total_row = jnp.sum(total * spread, axis=0, keepdims=True)
    skip_row = jnp.sum(skip * spread, axis=0, keepdims=True)
    for half in (0, 1):
        dmsg[half] = jnp.broadcast_to(total_row[:, half * 128 : half * 128 + 128], (8, 128))
    a2a_start(3, lambda k: dmsg.at[other(k) % 2], lambda k: drecv.at[seq])
    drecv[seq] = dmsg[c]
    use_mine(0, 3, 2)
    use_sib(0, 3, 2)
    ring_wait(1, 4)
    ring_wait(2, 4)
    sib_copy(0, 4).start()
    z_step(3, 2)
    z_step(4, 2)
    sib_copy(2, 0).start()
    mul_x(4)

    use_sib(0, 4, 1)
    x_b = xacc[...].astype(BF16)
    x_f = x_b.astype(F32)
    w_hi, w_lo = split(x_f * tail)

    bc_wait(0, bc_recv)
    b_t = bcbuf[0].reshape(STATE, TOK)
    end_state = dot(b_t, w_hi) + dot(b_t, w_lo)
    for s in range(SEQ):
        r, half = s // 2, s % 2
        cols = slice(half * 128, half * 128 + 128)
        smsg[s] = end_state[r * 16 : r * 16 + 16, cols]
    a2a_start(1, lambda k: smsg.at[other(k)], lambda k: srecv.at[seq])
    srecv[seq] = smsg[seq]

    for j in (2, 1, 3):
        bc_copy(1, j).start()
    z_step(3, 3)
    z_step(4, 3)
    bc_wait(1, bc_recv)
    c_m = bcbuf[1].reshape(STATE, TOK).astype(F32).T.astype(BF16)
    scores[...] = dot(c_m, b_t)
    ybuf[...] = x_f * skip_row

    def one_head(h, carry):
        pick = (iota((8, 128), 0) == h).astype(F32)
        rep = dot(cumt[...], pick, TN, HIGHEST)
        xm = jnp.where(iota((TOK, CH), 1) // HEAD_DIM == h, x_f, 0.0).astype(BF16)
        cum_row = cumt[pl.ds(h, 1), :]
        dt_row = dtt[pl.ds(h, 1), :]
        for i in range(4):
            highs, lows = [], []
            here = slice(i * 128, i * 128 + 128)
            for k in range(i + 1):
                cols = slice(k * 128, k * 128 + 128)
                between = rep[here, :] - cum_row[:, cols]
                if k == i:
                    between = jnp.where(iota((128, 128), 0) >= iota((128, 128), 1), between, -1e30)
                weight = scores[here, cols] * jnp.exp(between) * dt_row[:, cols]
                high, low = split(weight)
                highs.append(high)
                lows.append(low)
            if i:
                highs, lows = [jnp.concatenate(highs, axis=1)], [jnp.concatenate(lows, axis=1)]
            rows = xm[0 : i * 128 + 128, :]
            ybuf[here, :] += dot(highs[0], rows) + dot(lows[0], rows)
        return carry

    lax.fori_loop(0, LH, one_head, 0)
    a2a_wait(3, drecv.at[pl.ds(0, n_seq)])
    a2a_wait(1, srecv.at[pl.ds(0, n_seq)])

    def enter(s, carried):
        sout[s] = carried
        return jnp.exp(drecv[s][0:1, :]) * carried + srecv[s]

    lax.fori_loop(0, SEQ, enter, jnp.zeros((16, 128), F32))
    a2a_start(2, lambda k: sout.at[other(k)], lambda k: sin.at[seq])
    sin[seq] = sout[seq]
    mul_z(0)
    use_sib(2, 0, 1)
    use_mine(2, 1, 2)
    use_sib(2, 1, 2)

    use_mine(2, 2, 2)
    use_sib(2, 2, 2)
    loads[5].wait()
    at_col = iota((CH, NHEAD * 128), 1)
    wanted = (at_col // 128) * 64 + at_col % 128
    take = (at_col % 128 < 64) & (wanted == iota((CH, NHEAD * 128), 0))
    wpad[...] = dot(wout[...], take.astype(F32).astype(BF16)).astype(BF16)
    ring_wait(3, 4)
    ring_wait(4, 4)
    sib_copy(2, 4).start()
    use_mine(2, 3, 2)
    use_sib(2, 3, 2)
    mul_z(4)
    use_sib(2, 4, 1)
    z = zacc[...].astype(BF16).astype(F32)
    gate = z / (1.0 + jnp.exp(-z))

    a2a_start(0, lambda k: usrc.at[other(k)], lambda k: urecv.at[k])
    a2a_wait(2, sin.at[pl.ds(0, n_seq)])
    entering = jnp.concatenate(
        [jnp.concatenate([sin[2 * r], sin[2 * r + 1]], axis=1) for r in range(8)], axis=0
    )
    e_hi, e_lo = split(entering)
    gated = (ybuf[...] + ecum[...] * (dot(c_m, e_hi) + dot(c_m, e_lo))) * gate
    sq_hi, sq_lo = split(gated * gated)
    same = (iota((CH, CH), 0) // HEAD_DIM == iota((CH, CH), 1) // HEAD_DIM).astype(F32).astype(BF16)
    mean_sq = (dot(sq_hi, same) + dot(sq_lo, same)) * (1.0 / HEAD_DIM)
    normed = (gated * lax.rsqrt(mean_sq + 1e-05) * gain_ref[...]).astype(BF16)
    pooled = dot(ins[...].astype(BF16), normed) * span_inv
    psrc[0] = pooled[:, 0:128]
    psrc[1] = pooled[:, 128:256]

    def to_sibling(kind, src, dst):
        return pltpu.make_async_remote_copy(
            src_ref=src,
            dst_ref=dst,
            send_sem=p_send.at[kind],
            recv_sem=p_recv.at[kind],
            device_id={"seq": sibling},
            device_id_type=MESH,
        )

    first_half = to_sibling(0, psrc.at[1 - c], psib)
    first_half.start()
    first_half.wait_recv()
    pall[y] = (psrc[c] + psib[...]).astype(BF16)

    for k in range(RING - 1):
        peer = lax.rem(y + outward(k, RING // 2), RING) * 2 + c
        pltpu.make_async_remote_copy(
            src_ref=pall.at[y],
            dst_ref=pall.at[y],
            send_sem=p_send.at[1],
            recv_sem=p_recv.at[1],
            device_id={"seq": peer},
            device_id_type=MESH,
        ).start()

    most = pall.at[pl.ds(0, RING - 1)]
    pltpu.make_async_copy(most, most, p_recv.at[1]).wait()
    phalf[c] = jnp.sum(pall[...].astype(F32), axis=0)
    second_half = to_sibling(2, phalf.at[c], phalf.at[c])
    second_half.start()
    second_half.wait_recv()
    s_hi, s_lo = split(jnp.concatenate([phalf[0], phalf[1]], axis=1))
    slots = pick_slots[...].astype(BF16)
    value = dot(dot(slots, s_hi).astype(BF16), wpad[...]) + dot(
        dot(slots, s_lo).astype(BF16), wpad[...]
    )
    for o in range(NIVF):
        for h in range(NHEAD):
            fsrc[h * NIVF + o] = value[o * 8 : o * 8 + 8, h * 128 : h * 128 + 128]

    for k in range(n_far):
        h, o = far(k)
        pltpu.make_async_remote_copy(
            src_ref=fsrc.at[h * NIVF + o],
            dst_ref=frecv.at[k],
            send_sem=f_send,
            recv_sem=f_recv,
            device_id={"head": h, "ivf": o},
            device_id_type=MESH,
        ).start()

    def sent(d, carry):
        for n in range(5):
            for direction in (0, 1):
                if cuts[n][2 + direction] == 4:
                    ring_copy(n, direction, d).wait_send()
                else:

                    @pl.when(d < 3)
                    def _():
                        ring_copy(n, direction, d).wait_send()

        return carry

    def sib_sent(at, carry):
        for kind in range(3):
            sib_copy(kind, at).wait_send()
        return carry

    lax.fori_loop(0, 4, sent, 0)
    lax.fori_loop(0, 8, sib_sent, 0)
    bc_wait(0, bc_send)
    bc_wait(1, bc_send)
    a2a_sent(0, urecv)
    a2a_sent(1, srecv.at[pl.ds(0, n_seq)])
    a2a_sent(2, sin.at[pl.ds(0, n_seq)])
    a2a_sent(3, drecv.at[pl.ds(0, n_seq)])
    first_half.wait_send()
    second_half.wait_send()
    pltpu.make_async_copy(most, most, p_send.at[1]).wait()

    a2a_wait(0, urecv)
    mean_u = usrc[seq] + jnp.sum(urecv[...], axis=0)
    mean_u = jnp.where(head % 2 == 0, mean_u[:, 0:64], mean_u[:, 64:128])
    own = fsrc[head * NIVF + ivf]
    pltpu.make_async_copy(frecv, frecv, f_recv).wait()
    result = (own + jnp.sum(frecv[...], axis=0))[:, 0:64] + mean_u
    out_ref[0] = result[0:CAP, :]
    pltpu.make_async_copy(frecv, frecv, f_send).wait()


def local(
    hidden_in, w_x, w_z, w_dt, w_bc, dt_bias, a_rate, d_skip, norm_gain, w_out, span_lengths, owners
):
    any_spec = pl.BlockSpec(memory_space=pl.ANY)
    vmem_spec = pl.BlockSpec(memory_space=pltpu.VMEM)
    vmem = pltpu.VMEM
    dma = pltpu.SemaphoreType.DMA
    return pl.pallas_call(
        kernel,
        out_shape=jax.ShapeDtypeStruct((1, CAP, 64), F32),
        in_specs=[any_spec] * 12,
        out_specs=vmem_spec,
        scratch_shapes=[
            vmem((1, SPANS), jnp.int32),
            vmem((1, SPANS), jnp.int32),
            vmem((1, LH), F32),
            vmem((1, LH), F32),
            vmem((1, LH), F32),
            vmem((1, CH), F32),
            vmem((TOK, SEQ * KB), BF16),
            vmem((SEQ, AR, CH), BF16),
            vmem((SEQ, KB, CH), BF16),
            vmem((TOK, CH), F32),
            vmem((TOK, CH), F32),
            vmem((BCR + DTR, TOK), F32),
            vmem((2, SHARE, HALF, TOK), BF16),
            vmem((KB, 2 * STATE), BF16),
            vmem((LH, KB), BF16),
            vmem((CH, 256), BF16),
            vmem((CH, NHEAD * 128), BF16),
            vmem((64, SPANS), F32),
            vmem((SPANS, TOK), F32),
            vmem((SEQ, 8, 128), F32),
            vmem((SEQ - 1, 8, 128), F32),
            vmem((2, 8, 128), F32),
            vmem((SEQ, 8, 128), F32),
            vmem((SEQ, 16, 128), F32),
            vmem((SEQ, 16, 128), F32),
            vmem((SEQ, 16, 128), F32),
            vmem((SEQ, 16, 128), F32),
            vmem((TOK, TOK), F32),
            vmem((8, TOK), F32),
            vmem((8, TOK), F32),
            vmem((TOK, CH), F32),
            vmem((TOK, CH), F32),
            vmem((2, SPANS, 128), F32),
            vmem((SPANS, 128), F32),
            vmem((RING, SPANS, 128), BF16),
            vmem((2, SPANS, 128), F32),
            vmem((NHEAD * NIVF, 8, 128), F32),
            vmem((NHEAD * NIVF - 1, 8, 128), F32),
            dma((12,)),
            dma((5, 2, 4)),
            dma((5, 8)),
            dma((3, 8)),
            dma((3, 8)),
            dma((2,)),
            dma((2,)),
            dma((4,)),
            dma((4,)),
            dma((3,)),
            dma((3,)),
            dma,
            dma,
        ],
        compiler_params=pltpu.CompilerParams(
            collective_id=0, has_side_effects=True, vmem_limit_bytes=64 * 1024 * 1024
        ),
    )(
        hidden_in,
        w_x,
        w_z,
        w_dt.T,
        w_bc,
        w_out,
        span_lengths.reshape(1, SPANS),
        owners.T,
        dt_bias.reshape(1, LH),
        a_rate.reshape(1, LH),
        d_skip.reshape(1, LH),
        norm_gain.reshape(1, CH),
    )


def solution(mesh):
    return jax.shard_map(
        local,
        mesh=mesh,
        in_specs=(
            P("seq", None),
            P("seq", ("head", "ivf")),
            P("seq", ("head", "ivf")),
            P("seq", ("head", "ivf")),
            P("seq", "head"),
            P(("head", "ivf")),
            P(("head", "ivf")),
            P(("head", "ivf")),
            P(("head", "ivf")),
            P(("head", "ivf"), "seq"),
            P(),
            P(),
        ),
        out_specs=P("ivf", None, ("seq", "head")),
        check_vma=False,
    )
```

```python
import jax
import jax.numpy as jnp
from jax import lax
from jax.experimental import pallas as pl
from jax.experimental.pallas import tpu as pltpu
from jax.sharding import PartitionSpec as P

HEADS = 128
HEAD_DIM = 64
STATE = 128
GROUPS = 8
CAP = 6

SEQ = 16
RING = SEQ // 2
NHEAD = 4
NIVF = 8
TOK = 512
KB = 256
CH = 256
LH = CH // HEAD_DIM
SHARE = 4
BCR = 2 * STATE // SHARE
HALF = BCR // 2
DTR = 16
AR = KB + BCR + DTR
T_CUT = (KB, BCR + DTR, 4, 3)
X_CUTS = ((0, 128, 3, 4), (128, 128, 4, 3))
Z_CUTS = ((0, 128, 3, 4), (128, 128, 4, 3))
SPANS = 32
F32 = jnp.float32
BF16 = jnp.bfloat16
HIGHEST = lax.Precision.HIGHEST
MESH = pl.DeviceIdType.MESH

NN = (((1,), (0,)), ((), ()))
NT = (((1,), (1,)), ((), ()))
TN = (((0,), (0,)), ((), ()))


def dot(a, b, dims=NN, precision=None):
    return lax.dot_general(a, b, dims, precision=precision, preferred_element_type=F32)


def iota(shape, dim):
    return lax.broadcasted_iota(jnp.int32, shape, dim)


def split(v):
    high = v.astype(BF16)
    return high, (v - high.astype(F32)).astype(BF16)


def outward(k, middle):
    return middle + (1 - 2 * (k % 2)) * ((k + 1) // 2)


def lane_sums(v):
    width = v.shape[1]
    lane = iota(v.shape, 1)
    step = 1
    while step < width:
        v = v + jnp.where(lane >= step, pltpu.roll(v, step, 1), 0.0)
        step *= 2
    return v


def kernel(
    hid_hbm, wx_hbm, wz_hbm, wdt_hbm, wbc_hbm, wout_hbm,
    len_hbm, own_hbm, bias_hbm, rate_hbm, skip_hbm, gain_hbm,
    out_ref,
    len_ref, own_ref, bias_ref, rate_ref, skip_ref, gain_ref,
    hid, abuf, zbuf, xacc, zacc, bacc, bcbuf, wbc, wdt, wout, wpad, pick_slots, ins,
    usrc, urecv, dmsg, drecv, smsg, srecv, sout, sin, scores, cumt, dtt, ybuf, ecum,
    psrc, psib, pall, phalf, fsrc, frecv,
    ld_sem, ring_send, ring_recv, sib_send, sib_recv, bc_send, bc_recv,
    a2a_send, a2a_recv, p_send, p_recv, f_send, f_recv,
):
    seq = lax.axis_index("seq")
    head = lax.axis_index("head")
    ivf = lax.axis_index("ivf")
    y = seq // 2
    c = seq % 2
    up = ((y + 1) % RING) * 2 + c
    down = ((y + RING - 1) % RING) * 2 + c
    sibling = y * 2 + 1 - c
    piece = ivf % SHARE

    def other(k):
        return lax.rem(seq + outward(k, SEQ // 2), SEQ)

    def far(k):
        h = lax.rem(head + outward(k // NIVF, NHEAD // 2), NHEAD)
        o = lax.rem(ivf + outward(k % NIVF, NIVF // 2), NIVF)
        return h, o

    n_seq, n_far = SEQ - 1, NHEAD * NIVF - 1

    lanes = pl.ds(pl.multiple_of((ivf // SHARE) * (2 * STATE), 2 * STATE), 2 * STATE)
    loads = [
        pltpu.make_async_copy(wbc_hbm.at[:, lanes], wbc, ld_sem.at[0]),
        pltpu.make_async_copy(wdt_hbm, wdt, ld_sem.at[1]),
        pltpu.make_async_copy(wx_hbm, abuf.at[0, pl.ds(0, KB)], ld_sem.at[2]),
        pltpu.make_async_copy(wz_hbm, zbuf.at[0], ld_sem.at[3]),
        pltpu.make_async_copy(hid_hbm, hid, ld_sem.at[4]),
        pltpu.make_async_copy(wout_hbm, wout, ld_sem.at[5]),
        pltpu.make_async_copy(len_hbm, len_ref, ld_sem.at[6]),
        pltpu.make_async_copy(own_hbm, own_ref, ld_sem.at[7]),
        pltpu.make_async_copy(bias_hbm, bias_ref, ld_sem.at[8]),
        pltpu.make_async_copy(rate_hbm, rate_ref, ld_sem.at[9]),
        pltpu.make_async_copy(skip_hbm, skip_ref, ld_sem.at[10]),
        pltpu.make_async_copy(gain_hbm, gain_ref, ld_sem.at[11]),
    ]
    barrier = pltpu.get_barrier_semaphore()

    def greet_far(k, carry):
        h, o = far(k)
        pl.semaphore_signal(barrier, inc=1, device_id={"head": h, "ivf": o}, device_id_type=MESH)
        return carry

    def greet_seq(k, carry):
        pl.semaphore_signal(barrier, inc=1, device_id={"seq": other(k)}, device_id_type=MESH)
        return carry

    lax.fori_loop(0, n_far, greet_far, 0)
    lax.fori_loop(0, n_seq, greet_seq, 0)
    for load in loads:
        load.start()

    loads[0].wait()
    loads[1].wait()
    row = iota((BCR, 2 * STATE), 0)
    row = row + (row // HALF) * (STATE - HALF) + piece * HALF
    take = (row == iota((BCR, 2 * STATE), 1)).astype(F32).astype(BF16)
    abuf[0, KB : KB + BCR, :] = dot(take, wbc[...], NT).astype(BF16)
    take = (iota((DTR, LH), 0) == iota((DTR, LH), 1)).astype(F32).astype(BF16)
    abuf[0, KB + BCR : AR, :] = dot(take, wdt[...]).astype(BF16)
    loads[2].wait()
    pl.semaphore_wait(barrier, n_seq + n_far)

    cuts = (T_CUT,) + X_CUTS + Z_CUTS

    def ring_ref(n, at):
        buf = abuf if n < 3 else zbuf
        return buf.at[at, pl.ds(cuts[n][0], cuts[n][1])]

    def ring_copy(n, direction, d):
        if direction == 0:
            src, dst, peer = d, d + 1, up
        else:
            src, dst, peer = d + 4 * ((d + 3) // 4), d + 5 - 4 * (d // 3), down
        return pltpu.make_async_remote_copy(
            src_ref=ring_ref(n, src),
            dst_ref=ring_ref(n, dst),
            send_sem=ring_send.at[n, direction, d],
            recv_sem=ring_recv.at[n, dst],
            device_id={"seq": peer},
            device_id_type=MESH,
        )

    def ring_wait(n, at):
        ref = ring_ref(n, at)
        pltpu.make_async_copy(ref, ref, ring_recv.at[n, at]).wait()

    def sib_copy(kind, at):
        buf = (abuf, abuf, zbuf)[kind]
        rows = (pl.ds(0, KB), pl.ds(KB, AR - KB), pl.ds(0, KB))[kind]
        return pltpu.make_async_remote_copy(
            src_ref=buf.at[at, rows],
            dst_ref=buf.at[at + 8, rows],
            send_sem=sib_send.at[kind, at],
            recv_sem=sib_recv.at[kind, at],
            device_id={"seq": sibling},
            device_id_type=MESH,
        )

    def k_block(at):
        m = at % 8
        rel = (m // 5) * (2 * m - 4) - m
        side = at // 8
        core = c + side - 2 * c * side
        return ((y + rel + RING) % RING) * 2 + core

    def hid_cols(at):
        return hid[:, pl.ds(pl.multiple_of(k_block(at) * KB, KB), KB)]

    def mul_t(at):
        bacc[...] += dot(abuf[at, KB:AR, :], hid_cols(at), NT)

    def mul_x(at):
        xacc[...] += dot(hid_cols(at), abuf[at, 0:KB, :])

    def mul_z(at):
        zacc[...] += dot(hid_cols(at), zbuf[at])

    muls = (mul_x, mul_t, mul_z)

    def use_mine(kind, d, count):
        def one(i, carry):
            muls[kind](d + 4 * i)
            return carry

        lax.fori_loop(0, count, one, 0)

    def use_sib(kind, d, count):
        def one(i, carry):
            sib_copy(kind, d + 4 * i).wait_recv()
            muls[kind](8 + d + 4 * i)
            return carry

        lax.fori_loop(0, count, one, 0)

    for n in (0, 1, 2):
        ring_copy(n, 0, 0).start()
        ring_copy(n, 1, 0).start()
    sib_copy(1, 0).start()
    sib_copy(0, 0).start()
    xacc[...] = jnp.zeros_like(xacc)
    zacc[...] = jnp.zeros_like(zacc)
    bacc[...] = jnp.zeros_like(bacc)

    for load in loads[6:]:
        load.wait()
    lengths = jnp.broadcast_to(len_ref[...].astype(F32), (8, SPANS))
    ends = lengths
    step = 1
    while step < SPANS:
        moved = jnp.concatenate([jnp.zeros((8, step), F32), ends[:, : SPANS - step]], axis=1)
        ends = ends + moved
        step *= 2
    starts = ends - lengths
    member = (jnp.broadcast_to(own_ref[...], (8, SPANS)) == iota((8, SPANS), 0)).astype(F32)
    before = (iota((SPANS, SPANS), 0) < iota((SPANS, SPANS), 1)).astype(F32)
    rank = dot(member, before)
    slot = iota((8, SPANS), 0).astype(F32)
    pos = (iota((8, TOK), 1) + seq * TOK).astype(F32)
    own_first = jnp.zeros((8, 1), F32)
    own_last = jnp.zeros((8, 1), F32)
    for o in range(NIVF):
        chosen = jnp.where(rank[o : o + 1, :] == slot, member[o : o + 1, :], 0.0)
        pick_slots[o * 8 : o * 8 + 8, :] = chosen
        first = jnp.sum(chosen * starts, axis=1, keepdims=True)
        last = jnp.sum(chosen * ends, axis=1, keepdims=True)
        own_first = jnp.where(ivf == o, first, own_first)
        own_last = jnp.where(ivf == o, last, own_last)
    own_ins = ((pos >= own_first) & (pos < own_last)).astype(F32).astype(BF16)
    own_inv = 1.0 / jnp.maximum(own_last - own_first, 1.0)
    span_row = iota((SPANS, SPANS), 0) == iota((SPANS, SPANS), 1)
    span_first = jnp.sum(jnp.where(span_row, starts[0:1, :], 0.0), axis=1, keepdims=True)
    span_last = jnp.sum(jnp.where(span_row, ends[0:1, :], 0.0), axis=1, keepdims=True)
    span_pos = (iota((SPANS, TOK), 1) + seq * TOK).astype(F32)
    ins[...] = ((span_pos >= span_first) & (span_pos < span_last)).astype(F32)
    span_inv = 1.0 / (span_last - span_first)

    def a2a_start(kind, src_of, dst_of):
        for k in range(n_seq):
            pltpu.make_async_remote_copy(
                src_ref=src_of(k),
                dst_ref=dst_of(k),
                send_sem=a2a_send.at[kind],
                recv_sem=a2a_recv.at[kind],
                device_id={"seq": other(k)},
                device_id_type=MESH,
            ).start()

    def a2a_wait(kind, ref):
        pltpu.make_async_copy(ref, ref, a2a_recv.at[kind]).wait()

    def a2a_sent(kind, ref):
        pltpu.make_async_copy(ref, ref, a2a_send.at[kind]).wait()

    loads[3].wait()
    loads[4].wait()
    def u_block(s, carry):
        cols = pl.ds(pl.multiple_of(s * KB + (head // 2) * 128, 128), 128)
        usrc[s] = dot(own_ins, hid[:, cols]) * own_inv
        return carry

    lax.fori_loop(0, SEQ, u_block, 0)


    def z_start(n):
        ring_copy(n, 0, 0).start()
        ring_copy(n, 1, 0).start()

    def z_step(n, d):
        ring_wait(n, d)
        if d < cuts[n][2]:
            ring_copy(n, 0, d).start()
        ring_wait(n, 4 + d)
        if d < cuts[n][3]:
            ring_copy(n, 1, d).start()
        if n == 4:
            sib_copy(2, d).start()
            sib_copy(2, 4 + d).start()

    def a_step(d, carry):
        before = 1 + (d + 1) // 3
        ring_wait(0, d)
        ring_copy(0, 0, d).start()
        ring_wait(0, 4 + d)

        @pl.when(d < 3)
        def _():
            ring_copy(0, 1, d).start()

        sib_copy(1, d).start()
        sib_copy(1, 4 + d).start()
        use_mine(1, d - 1, before)
        use_mine(0, d - 1, before)
        ring_wait(1, 4 + d)
        ring_copy(1, 1, d).start()
        ring_wait(1, d)

        @pl.when(d < 3)
        def _():
            ring_copy(1, 0, d).start()

        use_sib(1, d - 1, before)
        use_sib(0, d - 1, before)
        ring_wait(2, d)
        ring_copy(2, 0, d).start()
        ring_wait(2, 4 + d)

        @pl.when(d < 3)
        def _():
            ring_copy(2, 1, d).start()

        sib_copy(0, d).start()
        sib_copy(0, 4 + d).start()

        @pl.when(d == 2)
        def _():
            z_start(3)
            z_start(4)

        @pl.when(d == 3)
        def _():
            z_step(3, 1)
            z_step(4, 1)

        return carry

    lax.fori_loop(1, 4, a_step, 0)
    ring_wait(0, 4)
    sib_copy(1, 4).start()
    use_mine(1, 3, 2)
    use_sib(1, 3, 2)
    mul_t(4)
    use_sib(1, 4, 1)

    for part in (0, 1):
        bcbuf[part, piece] = bacc[part * HALF : part * HALF + HALF, :].astype(BF16)

    def bc_copy(part, j):
        peer = (ivf // SHARE) * SHARE + lax.rem(piece + j, SHARE)
        return pltpu.make_async_remote_copy(
            src_ref=bcbuf.at[part, piece],
            dst_ref=bcbuf.at[part, piece],
            send_sem=bc_send.at[part],
            recv_sem=bc_recv.at[part],
            device_id={"ivf": peer},
            device_id_type=MESH,
        )

    def bc_wait(part, sem):
        ref = bcbuf.at[part, pl.ds(0, SHARE - 1)]
        pltpu.make_async_copy(ref, ref, sem.at[part]).wait()

    for j in (2, 1, 3):
        bc_copy(0, j).start()

    diag = iota((8, LH), 0) == iota((8, LH), 1)
    bias = jnp.sum(jnp.where(diag, bias_ref[...], 0.0), axis=1, keepdims=True)
    rate = jnp.sum(jnp.where(diag, rate_ref[...], 0.0), axis=1, keepdims=True)
    skip = jnp.sum(jnp.where(diag, skip_ref[...], 0.0), axis=1, keepdims=True)
    raw = bacc[BCR : BCR + 8, :] + bias
    step_size = jnp.maximum(raw, 0.0) + jnp.log1p(jnp.exp(-jnp.abs(raw)))
    cum = lane_sums(-step_size * rate)
    total = cum[:, TOK - 1 : TOK]
    cumt[...] = cum
    dtt[...] = step_size
    spread = (iota((8, CH), 1) // HEAD_DIM == iota((8, CH), 0)).astype(F32)
    tail = dot(jnp.exp(total - cum) * step_size, spread, TN, HIGHEST)
    ecum[...] = dot(jnp.exp(cum), spread, TN, HIGHEST)
    total_row = jnp.sum(total * spread, axis=0, keepdims=True)
    skip_row = jnp.sum(skip * spread, axis=0, keepdims=True)
    for half in (0, 1):
        dmsg[half] = jnp.broadcast_to(total_row[:, half * 128 : half * 128 + 128], (8, 128))
    a2a_start(3, lambda k: dmsg.at[other(k) % 2], lambda k: drecv.at[seq])
    drecv[seq] = dmsg[c]
    use_mine(0, 3, 2)
    use_sib(0, 3, 2)
    ring_wait(1, 4)
    ring_wait(2, 4)
    sib_copy(0, 4).start()
    z_step(3, 2)
    z_step(4, 2)
    sib_copy(2, 0).start()
    mul_x(4)

    use_sib(0, 4, 1)
    x_b = xacc[...].astype(BF16)
    x_f = x_b.astype(F32)
    w_hi, w_lo = split(x_f * tail)

    bc_wait(0, bc_recv)
    b_t = bcbuf[0].reshape(STATE, TOK)
    end_state = dot(b_t, w_hi) + dot(b_t, w_lo)
    for s in range(SEQ):
        r, half = s // 2, s % 2
        cols = slice(half * 128, half * 128 + 128)
        smsg[s] = end_state[r * 16 : r * 16 + 16, cols]
    a2a_start(1, lambda k: smsg.at[other(k)], lambda k: srecv.at[seq])
    srecv[seq] = smsg[seq]

    for j in (2, 1, 3):
        bc_copy(1, j).start()
    z_step(3, 3)
    z_step(4, 3)
    bc_wait(1, bc_recv)
    c_m = bcbuf[1].reshape(STATE, TOK).astype(F32).T.astype(BF16)
    scores[...] = dot(c_m, b_t)
    ybuf[...] = x_f * skip_row

    def one_head(h, carry):
        pick = (iota((8, 128), 0) == h).astype(F32)
        rep = dot(cumt[...], pick, TN, HIGHEST)
        xm = jnp.where(iota((TOK, CH), 1) // HEAD_DIM == h, x_f, 0.0).astype(BF16)
        cum_row = cumt[pl.ds(h, 1), :]
        dt_row = dtt[pl.ds(h, 1), :]
        for i in range(4):
            parts = []
            here = slice(i * 128, i * 128 + 128)
            for k in range(i + 1):
                cols = slice(k * 128, k * 128 + 128)
                between = rep[here, :] - cum_row[:, cols]
                if k == i:
                    between = jnp.where(iota((128, 128), 0) >= iota((128, 128), 1), between, -1e30)
                weight = scores[here, cols] * jnp.exp(between) * dt_row[:, cols]
                parts.append(weight.astype(BF16))
            block = jnp.concatenate(parts, axis=1) if i else parts[0]
            ybuf[here, :] += dot(block, xm[0 : i * 128 + 128, :])
        return carry

    lax.fori_loop(0, LH, one_head, 0)
    a2a_wait(3, drecv.at[pl.ds(0, n_seq)])
    a2a_wait(1, srecv.at[pl.ds(0, n_seq)])

    def enter(s, carried):
        sout[s] = carried
        return jnp.exp(drecv[s][0:1, :]) * carried + srecv[s]

    lax.fori_loop(0, SEQ, enter, jnp.zeros((16, 128), F32))
    a2a_start(2, lambda k: sout.at[other(k)], lambda k: sin.at[seq])
    sin[seq] = sout[seq]
    mul_z(0)
    use_sib(2, 0, 1)
    use_mine(2, 1, 2)
    use_sib(2, 1, 2)

    use_mine(2, 2, 2)
    use_sib(2, 2, 2)
    loads[5].wait()
    at_col = iota((CH, NHEAD * 128), 1)
    wanted = (at_col // 128) * 64 + at_col % 128
    take = (at_col % 128 < 64) & (wanted == iota((CH, NHEAD * 128), 0))
    wpad[...] = dot(wout[...], take.astype(F32).astype(BF16)).astype(BF16)
    ring_wait(3, 4)
    ring_wait(4, 4)
    sib_copy(2, 4).start()
    use_mine(2, 3, 2)
    use_sib(2, 3, 2)
    mul_z(4)
    use_sib(2, 4, 1)
    z = zacc[...].astype(BF16).astype(F32)
    gate = z / (1.0 + jnp.exp(-z))

    a2a_start(0, lambda k: usrc.at[other(k)], lambda k: urecv.at[k])
    a2a_wait(2, sin.at[pl.ds(0, n_seq)])
    entering = jnp.concatenate(
        [jnp.concatenate([sin[2 * r], sin[2 * r + 1]], axis=1) for r in range(8)], axis=0
    )
    e_hi, e_lo = split(entering)
    gated = (ybuf[...] + ecum[...] * (dot(c_m, e_hi) + dot(c_m, e_lo))) * gate
    sq_hi, sq_lo = split(gated * gated)
    same = (iota((CH, CH), 0) // HEAD_DIM == iota((CH, CH), 1) // HEAD_DIM).astype(F32).astype(BF16)
    mean_sq = (dot(sq_hi, same) + dot(sq_lo, same)) * (1.0 / HEAD_DIM)
    normed = (gated * lax.rsqrt(mean_sq + 1e-05) * gain_ref[...]).astype(BF16)
    pooled = dot(ins[...].astype(BF16), normed) * span_inv
    psrc[0] = pooled[:, 0:128]
    psrc[1] = pooled[:, 128:256]

    def to_sibling(kind, src, dst):
        return pltpu.make_async_remote_copy(
            src_ref=src,
            dst_ref=dst,
            send_sem=p_send.at[kind],
            recv_sem=p_recv.at[kind],
            device_id={"seq": sibling},
            device_id_type=MESH,
        )

    first_half = to_sibling(0, psrc.at[1 - c], psib)
    first_half.start()
    first_half.wait_recv()
    pall[y] = (psrc[c] + psib[...]).astype(BF16)

    for k in range(RING - 1):
        peer = lax.rem(y + outward(k, RING // 2), RING) * 2 + c
        pltpu.make_async_remote_copy(
            src_ref=pall.at[y],
            dst_ref=pall.at[y],
            send_sem=p_send.at[1],
            recv_sem=p_recv.at[1],
            device_id={"seq": peer},
            device_id_type=MESH,
        ).start()

    most = pall.at[pl.ds(0, RING - 1)]
    pltpu.make_async_copy(most, most, p_recv.at[1]).wait()
    phalf[c] = jnp.sum(pall[...].astype(F32), axis=0)
    second_half = to_sibling(2, phalf.at[c], phalf.at[c])
    second_half.start()
    second_half.wait_recv()
    s_hi, s_lo = split(jnp.concatenate([phalf[0], phalf[1]], axis=1))
    slots = pick_slots[...].astype(BF16)
    value = dot(dot(slots, s_hi).astype(BF16), wpad[...]) + dot(
        dot(slots, s_lo).astype(BF16), wpad[...]
    )
    for o in range(NIVF):
        for h in range(NHEAD):
            fsrc[h * NIVF + o] = value[o * 8 : o * 8 + 8, h * 128 : h * 128 + 128]

    for k in range(n_far):
        h, o = far(k)
        pltpu.make_async_remote_copy(
            src_ref=fsrc.at[h * NIVF + o],
            dst_ref=frecv.at[k],
            send_sem=f_send,
            recv_sem=f_recv,
            device_id={"head": h, "ivf": o},
            device_id_type=MESH,
        ).start()

    def sent(d, carry):
        for n in range(5):
            for direction in (0, 1):
                if cuts[n][2 + direction] == 4:
                    ring_copy(n, direction, d).wait_send()
                else:

                    @pl.when(d < 3)
                    def _():
                        ring_copy(n, direction, d).wait_send()

        return carry

    def sib_sent(at, carry):
        for kind in range(3):
            sib_copy(kind, at).wait_send()
        return carry

    lax.fori_loop(0, 4, sent, 0)
    lax.fori_loop(0, 8, sib_sent, 0)
    bc_wait(0, bc_send)
    bc_wait(1, bc_send)
    a2a_sent(0, urecv)
    a2a_sent(1, srecv.at[pl.ds(0, n_seq)])
    a2a_sent(2, sin.at[pl.ds(0, n_seq)])
    a2a_sent(3, drecv.at[pl.ds(0, n_seq)])
    first_half.wait_send()
    second_half.wait_send()
    pltpu.make_async_copy(most, most, p_send.at[1]).wait()

    a2a_wait(0, urecv)
    mean_u = usrc[seq] + jnp.sum(urecv[...], axis=0)
    mean_u = jnp.where(head % 2 == 0, mean_u[:, 0:64], mean_u[:, 64:128])
    own = fsrc[head * NIVF + ivf]
    pltpu.make_async_copy(frecv, frecv, f_recv).wait()
    result = (own + jnp.sum(frecv[...], axis=0))[:, 0:64] + mean_u
    out_ref[:, 0, :] = result[0:CAP, :]
    pltpu.make_async_copy(frecv, frecv, f_send).wait()


def local(
    hidden_in, w_x, w_z, w_dt, w_bc, dt_bias, a_rate, d_skip, norm_gain, w_out, span_lengths, owners
):
    any_spec = pl.BlockSpec(memory_space=pl.ANY)
    vmem_spec = pl.BlockSpec(memory_space=pltpu.VMEM)
    vmem = pltpu.VMEM
    dma = pltpu.SemaphoreType.DMA
    rows = pl.pallas_call(
        kernel,
        out_shape=jax.ShapeDtypeStruct((CAP, 1, 64), F32),
        in_specs=[any_spec] * 12,
        out_specs=vmem_spec,
        scratch_shapes=[
            vmem((1, SPANS), jnp.int32),
            vmem((1, SPANS), jnp.int32),
            vmem((1, LH), F32),
            vmem((1, LH), F32),
            vmem((1, LH), F32),
            vmem((1, CH), F32),
            vmem((TOK, SEQ * KB), BF16),
            vmem((SEQ, AR, CH), BF16),
            vmem((SEQ, KB, CH), BF16),
            vmem((TOK, CH), F32),
            vmem((TOK, CH), F32),
            vmem((BCR + DTR, TOK), F32),
            vmem((2, SHARE, HALF, TOK), BF16),
            vmem((KB, 2 * STATE), BF16),
            vmem((LH, KB), BF16),
            vmem((CH, 256), BF16),
            vmem((CH, NHEAD * 128), BF16),
            vmem((64, SPANS), F32),
            vmem((SPANS, TOK), F32),
            vmem((SEQ, 8, 128), F32),
            vmem((SEQ - 1, 8, 128), F32),
            vmem((2, 8, 128), F32),
            vmem((SEQ, 8, 128), F32),
            vmem((SEQ, 16, 128), F32),
            vmem((SEQ, 16, 128), F32),
            vmem((SEQ, 16, 128), F32),
            vmem((SEQ, 16, 128), F32),
            vmem((TOK, TOK), F32),
            vmem((8, TOK), F32),
            vmem((8, TOK), F32),
            vmem((TOK, CH), F32),
            vmem((TOK, CH), F32),
            vmem((2, SPANS, 128), F32),
            vmem((SPANS, 128), F32),
            vmem((RING, SPANS, 128), BF16),
            vmem((2, SPANS, 128), F32),
            vmem((NHEAD * NIVF, 8, 128), F32),
            vmem((NHEAD * NIVF - 1, 8, 128), F32),
            dma((12,)),
            dma((5, 2, 4)),
            dma((5, 8)),
            dma((3, 8)),
            dma((3, 8)),
            dma((2,)),
            dma((2,)),
            dma((4,)),
            dma((4,)),
            dma((3,)),
            dma((3,)),
            dma,
            dma,
        ],
        compiler_params=pltpu.CompilerParams(
            collective_id=0, has_side_effects=True, vmem_limit_bytes=64 * 1024 * 1024
        ),
    )(
        hidden_in,
        w_x,
        w_z,
        w_dt.T,
        w_bc,
        w_out,
        span_lengths.reshape(1, SPANS),
        owners.T,
        dt_bias.reshape(1, LH),
        a_rate.reshape(1, LH),
        d_skip.reshape(1, LH),
        norm_gain.reshape(1, CH),
    )
    return jnp.transpose(rows, (1, 0, 2))


def solution(mesh):
    return jax.shard_map(
        local,
        mesh=mesh,
        in_specs=(
            P("seq", None),
            P("seq", ("head", "ivf")),
            P("seq", ("head", "ivf")),
            P("seq", ("head", "ivf")),
            P("seq", "head"),
            P(("head", "ivf")),
            P(("head", "ivf")),
            P(("head", "ivf")),
            P(("head", "ivf")),
            P(("head", "ivf"), "seq"),
            P(),
            P(),
        ),
        out_specs=P("ivf", None, ("seq", "head")),
        check_vma=False,
    )
```

```python
import jax
import jax.numpy as jnp
from jax import lax
from jax.experimental import pallas as pl
from jax.experimental.pallas import tpu as pltpu
from jax.sharding import PartitionSpec as P

HEADS = 128
HEAD_DIM = 64
STATE = 128
GROUPS = 8
CAP = 6

SEQ = 16
RING = SEQ // 2
NHEAD = 4
NIVF = 8
TOK = 512
KB = 256
CH = 256
LH = CH // HEAD_DIM
SHARE = 4
BCR = 2 * STATE // SHARE
HALF = BCR // 2
DTR = 16
AR = KB + BCR + DTR
T_CUT = (KB, BCR + DTR, 4, 3)
X_CUTS = ((0, 128, 3, 4), (128, 128, 4, 3))
Z_CUTS = ((0, 128, 3, 4), (128, 128, 4, 3))
SPANS = 32
F32 = jnp.float32
BF16 = jnp.bfloat16
HIGHEST = lax.Precision.HIGHEST
MESH = pl.DeviceIdType.MESH

NN = (((1,), (0,)), ((), ()))
NT = (((1,), (1,)), ((), ()))
TN = (((0,), (0,)), ((), ()))


def dot(a, b, dims=NN, precision=None):
    return lax.dot_general(a, b, dims, precision=precision, preferred_element_type=F32)


def iota(shape, dim):
    return lax.broadcasted_iota(jnp.int32, shape, dim)


def split(v):
    high = v.astype(BF16)
    return high, (v - high.astype(F32)).astype(BF16)


def outward(k, middle):
    return middle + (1 - 2 * (k % 2)) * ((k + 1) // 2)


def lane_sums(v):
    width = v.shape[1]
    lane = iota(v.shape, 1)
    step = 1
    while step < width:
        v = v + jnp.where(lane >= step, pltpu.roll(v, step, 1), 0.0)
        step *= 2
    return v


def kernel(
    hid_hbm, wx_hbm, wz_hbm, wdt_hbm, wbc_hbm, wout_hbm,
    len_hbm, own_hbm, bias_hbm, rate_hbm, skip_hbm, gain_hbm,
    out_ref,
    len_ref, own_ref, bias_ref, rate_ref, skip_ref, gain_ref,
    hid, abuf, zbuf, xacc, zacc, bacc, bcbuf, wbc, wdt, wout, wpad, pick_slots, ins,
    usrc, urecv, dmsg, drecv, smsg, srecv, sout, sin, scores, cumt, dtt, ybuf, ecum,
    psrc, psib, pall, phalf, fsrc, frecv,
    ld_sem, ring_send, ring_recv, sib_send, sib_recv, bc_send, bc_recv,
    a2a_send, a2a_recv, p_send, p_recv, f_send, f_recv,
):
    seq = lax.axis_index("seq")
    head = lax.axis_index("head")
    ivf = lax.axis_index("ivf")
    y = seq // 2
    c = seq % 2
    up = ((y + 1) % RING) * 2 + c
    down = ((y + RING - 1) % RING) * 2 + c
    sibling = y * 2 + 1 - c
    piece = ivf % SHARE

    def other(k):
        return lax.rem(seq + outward(k, SEQ // 2), SEQ)

    def far(k):
        h = lax.rem(head + outward(k // NIVF, NHEAD // 2), NHEAD)
        o = lax.rem(ivf + outward(k % NIVF, NIVF // 2), NIVF)
        return h, o

    n_seq, n_far = SEQ - 1, NHEAD * NIVF - 1

    lanes = pl.ds(pl.multiple_of((ivf // SHARE) * (2 * STATE), 2 * STATE), 2 * STATE)
    loads = [
        pltpu.make_async_copy(wbc_hbm.at[:, lanes], wbc, ld_sem.at[0]),
        pltpu.make_async_copy(wdt_hbm, wdt, ld_sem.at[1]),
        pltpu.make_async_copy(wx_hbm, abuf.at[0, pl.ds(0, KB)], ld_sem.at[2]),
        pltpu.make_async_copy(wz_hbm, zbuf.at[0], ld_sem.at[3]),
        pltpu.make_async_copy(hid_hbm, hid, ld_sem.at[4]),
        pltpu.make_async_copy(wout_hbm, wout, ld_sem.at[5]),
        pltpu.make_async_copy(len_hbm, len_ref, ld_sem.at[6]),
        pltpu.make_async_copy(own_hbm, own_ref, ld_sem.at[7]),
        pltpu.make_async_copy(bias_hbm, bias_ref, ld_sem.at[8]),
        pltpu.make_async_copy(rate_hbm, rate_ref, ld_sem.at[9]),
        pltpu.make_async_copy(skip_hbm, skip_ref, ld_sem.at[10]),
        pltpu.make_async_copy(gain_hbm, gain_ref, ld_sem.at[11]),
    ]
    barrier = pltpu.get_barrier_semaphore()

    def greet_far(k, carry):
        h, o = far(k)
        pl.semaphore_signal(barrier, inc=1, device_id={"head": h, "ivf": o}, device_id_type=MESH)
        return carry

    def greet_seq(k, carry):
        pl.semaphore_signal(barrier, inc=1, device_id={"seq": other(k)}, device_id_type=MESH)
        return carry

    lax.fori_loop(0, n_far, greet_far, 0)
    lax.fori_loop(0, n_seq, greet_seq, 0)
    for load in loads:
        load.start()

    loads[0].wait()
    loads[1].wait()
    row = iota((BCR, 2 * STATE), 0)
    row = row + (row // HALF) * (STATE - HALF) + piece * HALF
    take = (row == iota((BCR, 2 * STATE), 1)).astype(F32).astype(BF16)
    abuf[0, KB : KB + BCR, :] = dot(take, wbc[...], NT).astype(BF16)
    take = (iota((DTR, LH), 0) == iota((DTR, LH), 1)).astype(F32).astype(BF16)
    abuf[0, KB + BCR : AR, :] = dot(take, wdt[...]).astype(BF16)
    loads[2].wait()
    pl.semaphore_wait(barrier, n_seq + n_far)

    cuts = (T_CUT,) + X_CUTS + Z_CUTS

    def ring_ref(n, at):
        buf = abuf if n < 3 else zbuf
        return buf.at[at, pl.ds(cuts[n][0], cuts[n][1])]

    def ring_copy(n, direction, d):
        if direction == 0:
            src, dst, peer = d, d + 1, up
        else:
            src, dst, peer = d + 4 * ((d + 3) // 4), d + 5 - 4 * (d // 3), down
        return pltpu.make_async_remote_copy(
            src_ref=ring_ref(n, src),
            dst_ref=ring_ref(n, dst),
            send_sem=ring_send.at[n, direction, d],
            recv_sem=ring_recv.at[n, dst],
            device_id={"seq": peer},
            device_id_type=MESH,
        )

    def ring_wait(n, at):
        ref = ring_ref(n, at)
        pltpu.make_async_copy(ref, ref, ring_recv.at[n, at]).wait()

    def sib_copy(kind, at):
        buf = (abuf, abuf, zbuf)[kind]
        rows = (pl.ds(0, KB), pl.ds(KB, AR - KB), pl.ds(0, KB))[kind]
        return pltpu.make_async_remote_copy(
            src_ref=buf.at[at, rows],
            dst_ref=buf.at[at + 8, rows],
            send_sem=sib_send.at[kind, at],
            recv_sem=sib_recv.at[kind, at],
            device_id={"seq": sibling},
            device_id_type=MESH,
        )

    def k_block(at):
        m = at % 8
        rel = (m // 5) * (2 * m - 4) - m
        side = at // 8
        core = c + side - 2 * c * side
        return ((y + rel + RING) % RING) * 2 + core

    def hid_cols(at):
        return hid[:, pl.ds(pl.multiple_of(k_block(at) * KB, KB), KB)]

    def mul_t(at):
        bacc[...] += dot(abuf[at, KB:AR, :], hid_cols(at), NT)

    def mul_x(at):
        xacc[...] += dot(hid_cols(at), abuf[at, 0:KB, :])

    def mul_z(at):
        zacc[...] += dot(hid_cols(at), zbuf[at])

    muls = (mul_x, mul_t, mul_z)

    def use_mine(kind, d, count):
        def one(i, carry):
            muls[kind](d + 4 * i)
            return carry

        lax.fori_loop(0, count, one, 0)

    def use_sib(kind, d, count):
        def one(i, carry):
            sib_copy(kind, d + 4 * i).wait_recv()
            muls[kind](8 + d + 4 * i)
            return carry

        lax.fori_loop(0, count, one, 0)

    for n in (0, 1, 2):
        ring_copy(n, 0, 0).start()
        ring_copy(n, 1, 0).start()
    sib_copy(1, 0).start()
    sib_copy(0, 0).start()
    xacc[...] = jnp.zeros_like(xacc)
    zacc[...] = jnp.zeros_like(zacc)
    bacc[...] = jnp.zeros_like(bacc)

    for load in loads[6:]:
        load.wait()
    lengths = jnp.broadcast_to(len_ref[...].astype(F32), (8, SPANS))
    ends = lengths
    step = 1
    while step < SPANS:
        moved = jnp.concatenate([jnp.zeros((8, step), F32), ends[:, : SPANS - step]], axis=1)
        ends = ends + moved
        step *= 2
    starts = ends - lengths
    member = (jnp.broadcast_to(own_ref[...], (8, SPANS)) == iota((8, SPANS), 0)).astype(F32)
    before = (iota((SPANS, SPANS), 0) < iota((SPANS, SPANS), 1)).astype(F32)
    rank = dot(member, before)
    slot = iota((8, SPANS), 0).astype(F32)
    pos = (iota((8, TOK), 1) + seq * TOK).astype(F32)
    own_first = jnp.zeros((8, 1), F32)
    own_last = jnp.zeros((8, 1), F32)
    for o in range(NIVF):
        chosen = jnp.where(rank[o : o + 1, :] == slot, member[o : o + 1, :], 0.0)
        pick_slots[o * 8 : o * 8 + 8, :] = chosen
        first = jnp.sum(chosen * starts, axis=1, keepdims=True)
        last = jnp.sum(chosen * ends, axis=1, keepdims=True)
        own_first = jnp.where(ivf == o, first, own_first)
        own_last = jnp.where(ivf == o, last, own_last)
    own_ins = ((pos >= own_first) & (pos < own_last)).astype(F32).astype(BF16)
    own_inv = 1.0 / jnp.maximum(own_last - own_first, 1.0)
    span_row = iota((SPANS, SPANS), 0) == iota((SPANS, SPANS), 1)
    span_first = jnp.sum(jnp.where(span_row, starts[0:1, :], 0.0), axis=1, keepdims=True)
    span_last = jnp.sum(jnp.where(span_row, ends[0:1, :], 0.0), axis=1, keepdims=True)
    span_pos = (iota((SPANS, TOK), 1) + seq * TOK).astype(F32)
    ins[...] = ((span_pos >= span_first) & (span_pos < span_last)).astype(F32)
    span_inv = 1.0 / (span_last - span_first)

    def a2a_start(kind, src_of, dst_of):
        for k in range(n_seq):
            pltpu.make_async_remote_copy(
                src_ref=src_of(k),
                dst_ref=dst_of(k),
                send_sem=a2a_send.at[kind],
                recv_sem=a2a_recv.at[kind],
                device_id={"seq": other(k)},
                device_id_type=MESH,
            ).start()

    def a2a_wait(kind, ref):
        pltpu.make_async_copy(ref, ref, a2a_recv.at[kind]).wait()

    def a2a_sent(kind, ref):
        pltpu.make_async_copy(ref, ref, a2a_send.at[kind]).wait()

    loads[3].wait()
    loads[4].wait()
    def u_block(s, carry):
        cols = pl.ds(pl.multiple_of(s * KB + (head // 2) * 128, 128), 128)
        usrc[s] = dot(own_ins, hid[:, cols]) * own_inv
        return carry

    lax.fori_loop(0, SEQ, u_block, 0)


    def z_start(n):
        ring_copy(n, 0, 0).start()
        ring_copy(n, 1, 0).start()

    def z_step(n, d):
        ring_wait(n, d)
        if d < cuts[n][2]:
            ring_copy(n, 0, d).start()
        ring_wait(n, 4 + d)
        if d < cuts[n][3]:
            ring_copy(n, 1, d).start()
        if n == 4:
            sib_copy(2, d).start()
            sib_copy(2, 4 + d).start()

    def a_step(d, carry):
        before = 1 + (d + 1) // 3
        ring_wait(0, d)
        ring_copy(0, 0, d).start()
        ring_wait(0, 4 + d)

        @pl.when(d < 3)
        def _():
            ring_copy(0, 1, d).start()

        sib_copy(1, d).start()
        sib_copy(1, 4 + d).start()
        use_mine(1, d - 1, before)
        use_mine(0, d - 1, before)
        ring_wait(1, 4 + d)
        ring_copy(1, 1, d).start()
        ring_wait(1, d)

        @pl.when(d < 3)
        def _():
            ring_copy(1, 0, d).start()

        use_sib(1, d - 1, before)
        use_sib(0, d - 1, before)
        ring_wait(2, d)
        ring_copy(2, 0, d).start()
        ring_wait(2, 4 + d)

        @pl.when(d < 3)
        def _():
            ring_copy(2, 1, d).start()

        sib_copy(0, d).start()
        sib_copy(0, 4 + d).start()

        @pl.when(d == 3)
        def _():
            z_start(3)
            z_start(4)

        return carry

    lax.fori_loop(1, 4, a_step, 0)
    ring_wait(0, 4)
    sib_copy(1, 4).start()
    use_mine(1, 3, 2)
    use_sib(1, 3, 2)
    mul_t(4)
    use_sib(1, 4, 1)

    for part in (0, 1):
        bcbuf[part, piece] = bacc[part * HALF : part * HALF + HALF, :].astype(BF16)

    def bc_copy(part, j):
        peer = (ivf // SHARE) * SHARE + lax.rem(piece + j, SHARE)
        return pltpu.make_async_remote_copy(
            src_ref=bcbuf.at[part, piece],
            dst_ref=bcbuf.at[part, piece],
            send_sem=bc_send.at[part],
            recv_sem=bc_recv.at[part],
            device_id={"ivf": peer},
            device_id_type=MESH,
        )

    def bc_wait(part, sem):
        ref = bcbuf.at[part, pl.ds(0, SHARE - 1)]
        pltpu.make_async_copy(ref, ref, sem.at[part]).wait()

    for j in (2, 1, 3):
        bc_copy(0, j).start()

    diag = iota((8, LH), 0) == iota((8, LH), 1)
    bias = jnp.sum(jnp.where(diag, bias_ref[...], 0.0), axis=1, keepdims=True)
    rate = jnp.sum(jnp.where(diag, rate_ref[...], 0.0), axis=1, keepdims=True)
    skip = jnp.sum(jnp.where(diag, skip_ref[...], 0.0), axis=1, keepdims=True)
    raw = bacc[BCR : BCR + 8, :] + bias
    step_size = jnp.maximum(raw, 0.0) + jnp.log1p(jnp.exp(-jnp.abs(raw)))
    cum = lane_sums(-step_size * rate)
    total = cum[:, TOK - 1 : TOK]
    cumt[...] = cum
    dtt[...] = step_size
    spread = (iota((8, CH), 1) // HEAD_DIM == iota((8, CH), 0)).astype(F32)
    tail = dot(jnp.exp(total - cum) * step_size, spread, TN, HIGHEST)
    ecum[...] = dot(jnp.exp(cum), spread, TN, HIGHEST)
    total_row = jnp.sum(total * spread, axis=0, keepdims=True)
    skip_row = jnp.sum(skip * spread, axis=0, keepdims=True)
    for half in (0, 1):
        dmsg[half] = jnp.broadcast_to(total_row[:, half * 128 : half * 128 + 128], (8, 128))
    a2a_start(3, lambda k: dmsg.at[other(k) % 2], lambda k: drecv.at[seq])
    drecv[seq] = dmsg[c]
    use_mine(0, 3, 2)
    use_sib(0, 3, 2)
    ring_wait(1, 4)
    ring_wait(2, 4)
    sib_copy(0, 4).start()
    z_step(3, 1)
    z_step(4, 1)
    sib_copy(2, 0).start()
    mul_x(4)

    use_sib(0, 4, 1)
    x_b = xacc[...].astype(BF16)
    x_f = x_b.astype(F32)
    w_hi, w_lo = split(x_f * tail)

    bc_wait(0, bc_recv)
    b_t = bcbuf[0].reshape(STATE, TOK)
    end_state = dot(b_t, w_hi) + dot(b_t, w_lo)
    for s in range(SEQ):
        r, half = s // 2, s % 2
        cols = slice(half * 128, half * 128 + 128)
        smsg[s] = end_state[r * 16 : r * 16 + 16, cols]
    a2a_start(1, lambda k: smsg.at[other(k)], lambda k: srecv.at[seq])
    srecv[seq] = smsg[seq]

    for j in (2, 1, 3):
        bc_copy(1, j).start()
    z_step(3, 2)
    z_step(4, 2)
    bc_wait(1, bc_recv)
    c_m = bcbuf[1].reshape(STATE, TOK).astype(F32).T.astype(BF16)
    scores[...] = dot(c_m, b_t)
    ybuf[...] = x_f * skip_row

    def one_head(h, carry):
        pick = (iota((8, 128), 0) == h).astype(F32)
        rep = dot(cumt[...], pick, TN, HIGHEST)
        xm = jnp.where(iota((TOK, CH), 1) // HEAD_DIM == h, x_f, 0.0).astype(BF16)
        cum_row = cumt[pl.ds(h, 1), :]
        dt_row = dtt[pl.ds(h, 1), :]
        for i in range(4):
            parts = []
            here = slice(i * 128, i * 128 + 128)
            for k in range(i + 1):
                cols = slice(k * 128, k * 128 + 128)
                between = rep[here, :] - cum_row[:, cols]
                if k == i:
                    between = jnp.where(iota((128, 128), 0) >= iota((128, 128), 1), between, -1e30)
                weight = scores[here, cols] * jnp.exp(between) * dt_row[:, cols]
                parts.append(weight.astype(BF16))
            block = jnp.concatenate(parts, axis=1) if i else parts[0]
            ybuf[here, :] += dot(block, xm[0 : i * 128 + 128, :])
        return carry

    lax.fori_loop(0, LH, one_head, 0)
    a2a_wait(3, drecv.at[pl.ds(0, n_seq)])
    a2a_wait(1, srecv.at[pl.ds(0, n_seq)])

    def enter(s, carried):
        sout[s] = carried
        return jnp.exp(drecv[s][0:1, :]) * carried + srecv[s]

    lax.fori_loop(0, SEQ, enter, jnp.zeros((16, 128), F32))
    a2a_start(2, lambda k: sout.at[other(k)], lambda k: sin.at[seq])
    sin[seq] = sout[seq]
    z_step(3, 3)
    z_step(4, 3)
    mul_z(0)
    use_sib(2, 0, 1)
    use_mine(2, 1, 2)
    use_sib(2, 1, 2)

    use_mine(2, 2, 2)
    use_sib(2, 2, 2)
    loads[5].wait()
    at_col = iota((CH, NHEAD * 128), 1)
    wanted = (at_col // 128) * 64 + at_col % 128
    take = (at_col % 128 < 64) & (wanted == iota((CH, NHEAD * 128), 0))
    wpad[...] = dot(wout[...], take.astype(F32).astype(BF16)).astype(BF16)
    ring_wait(3, 4)
    ring_wait(4, 4)
    sib_copy(2, 4).start()
    use_mine(2, 3, 2)
    use_sib(2, 3, 2)
    mul_z(4)
    use_sib(2, 4, 1)
    z = zacc[...].astype(BF16).astype(F32)
    gate = z / (1.0 + jnp.exp(-z))

    a2a_start(0, lambda k: usrc.at[other(k)], lambda k: urecv.at[k])
    a2a_wait(2, sin.at[pl.ds(0, n_seq)])
    entering = jnp.concatenate(
        [jnp.concatenate([sin[2 * r], sin[2 * r + 1]], axis=1) for r in range(8)], axis=0
    )
    e_hi, e_lo = split(entering)
    gated = (ybuf[...] + ecum[...] * (dot(c_m, e_hi) + dot(c_m, e_lo))) * gate
    square = (gated * gated).astype(BF16)
    same = (iota((CH, CH), 0) // HEAD_DIM == iota((CH, CH), 1) // HEAD_DIM).astype(F32).astype(BF16)
    mean_sq = dot(square, same) * (1.0 / HEAD_DIM)
    normed = (gated * lax.rsqrt(mean_sq + 1e-05) * gain_ref[...]).astype(BF16)
    pooled = dot(ins[...].astype(BF16), normed) * span_inv
    psrc[0] = pooled[:, 0:128]
    psrc[1] = pooled[:, 128:256]

    def to_sibling(kind, src, dst):
        return pltpu.make_async_remote_copy(
            src_ref=src,
            dst_ref=dst,
            send_sem=p_send.at[kind],
            recv_sem=p_recv.at[kind],
            device_id={"seq": sibling},
            device_id_type=MESH,
        )

    first_half = to_sibling(0, psrc.at[1 - c], psib)
    first_half.start()
    first_half.wait_recv()
    pall[y] = (psrc[c] + psib[...]).astype(BF16)

    for k in range(RING - 1):
        peer = lax.rem(y + outward(k, RING // 2), RING) * 2 + c
        pltpu.make_async_remote_copy(
            src_ref=pall.at[y],
            dst_ref=pall.at[y],
            send_sem=p_send.at[1],
            recv_sem=p_recv.at[1],
            device_id={"seq": peer},
            device_id_type=MESH,
        ).start()

    most = pall.at[pl.ds(0, RING - 1)]
    pltpu.make_async_copy(most, most, p_recv.at[1]).wait()
    phalf[c] = jnp.sum(pall[...].astype(F32), axis=0)
    second_half = to_sibling(2, phalf.at[c], phalf.at[c])
    second_half.start()
    second_half.wait_recv()
    s_hi, s_lo = split(jnp.concatenate([phalf[0], phalf[1]], axis=1))
    slots = pick_slots[...].astype(BF16)
    value = dot(dot(slots, s_hi).astype(BF16), wpad[...]) + dot(
        dot(slots, s_lo).astype(BF16), wpad[...]
    )
    for o in range(NIVF):
        for h in range(NHEAD):
            fsrc[h * NIVF + o] = value[o * 8 : o * 8 + 8, h * 128 : h * 128 + 128]

    for k in range(n_far):
        h, o = far(k)
        pltpu.make_async_remote_copy(
            src_ref=fsrc.at[h * NIVF + o],
            dst_ref=frecv.at[k],
            send_sem=f_send,
            recv_sem=f_recv,
            device_id={"head": h, "ivf": o},
            device_id_type=MESH,
        ).start()

    def sent(d, carry):
        for n in range(5):
            for direction in (0, 1):
                if cuts[n][2 + direction] == 4:
                    ring_copy(n, direction, d).wait_send()
                else:

                    @pl.when(d < 3)
                    def _():
                        ring_copy(n, direction, d).wait_send()

        return carry

    def sib_sent(at, carry):
        for kind in range(3):
            sib_copy(kind, at).wait_send()
        return carry

    lax.fori_loop(0, 4, sent, 0)
    lax.fori_loop(0, 8, sib_sent, 0)
    bc_wait(0, bc_send)
    bc_wait(1, bc_send)
    a2a_sent(0, urecv)
    a2a_sent(1, srecv.at[pl.ds(0, n_seq)])
    a2a_sent(2, sin.at[pl.ds(0, n_seq)])
    a2a_sent(3, drecv.at[pl.ds(0, n_seq)])
    first_half.wait_send()
    second_half.wait_send()
    pltpu.make_async_copy(most, most, p_send.at[1]).wait()

    a2a_wait(0, urecv)
    mean_u = usrc[seq] + jnp.sum(urecv[...], axis=0)
    mean_u = jnp.where(head % 2 == 0, mean_u[:, 0:64], mean_u[:, 64:128])
    own = fsrc[head * NIVF + ivf]
    pltpu.make_async_copy(frecv, frecv, f_recv).wait()
    result = (own + jnp.sum(frecv[...], axis=0))[:, 0:64] + mean_u
    out_ref[:, 0, :] = result[0:CAP, :]
    pltpu.make_async_copy(frecv, frecv, f_send).wait()


def local(
    hidden_in, w_x, w_z, w_dt, w_bc, dt_bias, a_rate, d_skip, norm_gain, w_out, span_lengths, owners
):
    any_spec = pl.BlockSpec(memory_space=pl.ANY)
    vmem_spec = pl.BlockSpec(memory_space=pltpu.VMEM)
    vmem = pltpu.VMEM
    dma = pltpu.SemaphoreType.DMA
    rows = pl.pallas_call(
        kernel,
        out_shape=jax.ShapeDtypeStruct((CAP, 1, 64), F32),
        in_specs=[any_spec] * 12,
        out_specs=vmem_spec,
        scratch_shapes=[
            vmem((1, SPANS), jnp.int32),
            vmem((1, SPANS), jnp.int32),
            vmem((1, LH), F32),
            vmem((1, LH), F32),
            vmem((1, LH), F32),
            vmem((1, CH), F32),
            vmem((TOK, SEQ * KB), BF16),
            vmem((SEQ, AR, CH), BF16),
            vmem((SEQ, KB, CH), BF16),
            vmem((TOK, CH), F32),
            vmem((TOK, CH), F32),
            vmem((BCR + DTR, TOK), F32),
            vmem((2, SHARE, HALF, TOK), BF16),
            vmem((KB, 2 * STATE), BF16),
            vmem((LH, KB), BF16),
            vmem((CH, 256), BF16),
            vmem((CH, NHEAD * 128), BF16),
            vmem((64, SPANS), F32),
            vmem((SPANS, TOK), F32),
            vmem((SEQ, 8, 128), F32),
            vmem((SEQ - 1, 8, 128), F32),
            vmem((2, 8, 128), F32),
            vmem((SEQ, 8, 128), F32),
            vmem((SEQ, 16, 128), F32),
            vmem((SEQ, 16, 128), F32),
            vmem((SEQ, 16, 128), F32),
            vmem((SEQ, 16, 128), F32),
            vmem((TOK, TOK), F32),
            vmem((8, TOK), F32),
            vmem((8, TOK), F32),
            vmem((TOK, CH), F32),
            vmem((TOK, CH), F32),
            vmem((2, SPANS, 128), F32),
            vmem((SPANS, 128), F32),
            vmem((RING, SPANS, 128), BF16),
            vmem((2, SPANS, 128), F32),
            vmem((NHEAD * NIVF, 8, 128), F32),
            vmem((NHEAD * NIVF - 1, 8, 128), F32),
            dma((12,)),
            dma((5, 2, 4)),
            dma((5, 8)),
            dma((3, 8)),
            dma((3, 8)),
            dma((2,)),
            dma((2,)),
            dma((4,)),
            dma((4,)),
            dma((3,)),
            dma((3,)),
            dma,
            dma,
        ],
        compiler_params=pltpu.CompilerParams(
            collective_id=0, has_side_effects=True, vmem_limit_bytes=64 * 1024 * 1024
        ),
    )(
        hidden_in,
        w_x,
        w_z,
        w_dt.T,
        w_bc,
        w_out,
        span_lengths.reshape(1, SPANS),
        owners.T,
        dt_bias.reshape(1, LH),
        a_rate.reshape(1, LH),
        d_skip.reshape(1, LH),
        norm_gain.reshape(1, CH),
    )
    return jnp.transpose(rows, (1, 0, 2))


def solution(mesh):
    return jax.shard_map(
        local,
        mesh=mesh,
        in_specs=(
            P("seq", None),
            P("seq", ("head", "ivf")),
            P("seq", ("head", "ivf")),
            P("seq", ("head", "ivf")),
            P("seq", "head"),
            P(("head", "ivf")),
            P(("head", "ivf")),
            P(("head", "ivf")),
            P(("head", "ivf")),
            P(("head", "ivf"), "seq"),
            P(),
            P(),
        ),
        out_specs=P("ivf", None, ("seq", "head")),
        check_vma=False,
    )
```

```python
import jax
import jax.numpy as jnp
from jax import lax
from jax.experimental import pallas as pl
from jax.experimental.pallas import tpu as pltpu
from jax.sharding import PartitionSpec as P

HEADS = 128
HEAD_DIM = 64
STATE = 128
GROUPS = 8
CAP = 6

SEQ = 16
RING = SEQ // 2
NHEAD = 4
NIVF = 8
TOK = 512
KB = 256
CH = 256
LH = CH // HEAD_DIM
SHARE = 4
BCR = 2 * STATE // SHARE
HALF = BCR // 2
DTR = 16
AR = KB + BCR + DTR
T_CUT = (KB, BCR + DTR, 4, 3)
X_CUTS = ((0, 128, 3, 4), (128, 128, 4, 3))
Z_CUTS = ((0, 128, 3, 4), (128, 128, 4, 3))
SPANS = 32
F32 = jnp.float32
BF16 = jnp.bfloat16
HIGHEST = lax.Precision.HIGHEST
MESH = pl.DeviceIdType.MESH

NN = (((1,), (0,)), ((), ()))
NT = (((1,), (1,)), ((), ()))
TN = (((0,), (0,)), ((), ()))


def dot(a, b, dims=NN, precision=None):
    return lax.dot_general(a, b, dims, precision=precision, preferred_element_type=F32)


def iota(shape, dim):
    return lax.broadcasted_iota(jnp.int32, shape, dim)


def split(v):
    high = v.astype(BF16)
    return high, (v - high.astype(F32)).astype(BF16)


def outward(k, middle):
    return middle + (1 - 2 * (k % 2)) * ((k + 1) // 2)


def lane_sums(v):
    width = v.shape[1]
    lane = iota(v.shape, 1)
    step = 1
    while step < width:
        v = v + jnp.where(lane >= step, pltpu.roll(v, step, 1), 0.0)
        step *= 2
    return v


def kernel(
    hid_hbm, wx_hbm, wz_hbm, wdt_hbm, wbc_hbm, wout_hbm,
    len_hbm, own_hbm, bias_hbm, rate_hbm, skip_hbm, gain_hbm,
    out_ref,
    len_ref, own_ref, bias_ref, rate_ref, skip_ref, gain_ref,
    hid, abuf, zbuf, xacc, zacc, bacc, bcbuf, wbc, wdt, wout, wpad, pick_slots, ins,
    usrc, urecv, dmsg, drecv, smsg, srecv, sout, sin, scores, cumt, dtt, ybuf, ecum,
    psrc, psib, pall, phalf, fsrc, frecv,
    ld_sem, ring_send, ring_recv, sib_send, sib_recv, bc_send, bc_recv,
    a2a_send, a2a_recv, p_send, p_recv, f_send, f_recv,
):
    seq = lax.axis_index("seq")
    head = lax.axis_index("head")
    ivf = lax.axis_index("ivf")
    y = seq // 2
    c = seq % 2
    up = ((y + 1) % RING) * 2 + c
    down = ((y + RING - 1) % RING) * 2 + c
    sibling = y * 2 + 1 - c
    piece = ivf % SHARE

    def other(k):
        return lax.rem(seq + outward(k, SEQ // 2), SEQ)

    def far(k):
        h = lax.rem(head + outward(k // NIVF, NHEAD // 2), NHEAD)
        o = lax.rem(ivf + outward(k % NIVF, NIVF // 2), NIVF)
        return h, o

    n_seq, n_far = SEQ - 1, NHEAD * NIVF - 1

    lanes = pl.ds(pl.multiple_of((ivf // SHARE) * (2 * STATE), 2 * STATE), 2 * STATE)
    loads = [
        pltpu.make_async_copy(wbc_hbm.at[:, lanes], wbc, ld_sem.at[0]),
        pltpu.make_async_copy(wdt_hbm, wdt, ld_sem.at[1]),
        pltpu.make_async_copy(wx_hbm, abuf.at[0, pl.ds(0, KB)], ld_sem.at[2]),
        pltpu.make_async_copy(wz_hbm, zbuf.at[0], ld_sem.at[3]),
        pltpu.make_async_copy(hid_hbm, hid, ld_sem.at[4]),
        pltpu.make_async_copy(wout_hbm, wout, ld_sem.at[5]),
        pltpu.make_async_copy(len_hbm, len_ref, ld_sem.at[6]),
        pltpu.make_async_copy(own_hbm, own_ref, ld_sem.at[7]),
        pltpu.make_async_copy(bias_hbm, bias_ref, ld_sem.at[8]),
        pltpu.make_async_copy(rate_hbm, rate_ref, ld_sem.at[9]),
        pltpu.make_async_copy(skip_hbm, skip_ref, ld_sem.at[10]),
        pltpu.make_async_copy(gain_hbm, gain_ref, ld_sem.at[11]),
    ]
    barrier = pltpu.get_barrier_semaphore()

    def greet_far(k, carry):
        h, o = far(k)
        pl.semaphore_signal(barrier, inc=1, device_id={"head": h, "ivf": o}, device_id_type=MESH)
        return carry

    def greet_seq(k, carry):
        pl.semaphore_signal(barrier, inc=1, device_id={"seq": other(k)}, device_id_type=MESH)
        return carry

    lax.fori_loop(0, n_far, greet_far, 0)
    lax.fori_loop(0, n_seq, greet_seq, 0)
    for load in loads:
        load.start()

    loads[0].wait()
    loads[1].wait()
    row = iota((BCR, 2 * STATE), 0)
    row = row + (row // HALF) * (STATE - HALF) + piece * HALF
    take = (row == iota((BCR, 2 * STATE), 1)).astype(F32).astype(BF16)
    abuf[0, KB : KB + BCR, :] = dot(take, wbc[...], NT).astype(BF16)
    take = (iota((DTR, LH), 0) == iota((DTR, LH), 1)).astype(F32).astype(BF16)
    abuf[0, KB + BCR : AR, :] = dot(take, wdt[...]).astype(BF16)
    loads[2].wait()
    pl.semaphore_wait(barrier, n_seq + n_far)

    cuts = (T_CUT,) + X_CUTS + Z_CUTS

    def ring_ref(n, at):
        buf = abuf if n < 3 else zbuf
        return buf.at[at, pl.ds(cuts[n][0], cuts[n][1])]

    def ring_copy(n, direction, d):
        if direction == 0:
            src, dst, peer = d, d + 1, up
        else:
            src, dst, peer = d + 4 * ((d + 3) // 4), d + 5 - 4 * (d // 3), down
        return pltpu.make_async_remote_copy(
            src_ref=ring_ref(n, src),
            dst_ref=ring_ref(n, dst),
            send_sem=ring_send.at[n, direction, d],
            recv_sem=ring_recv.at[n, dst],
            device_id={"seq": peer},
            device_id_type=MESH,
        )

    def ring_wait(n, at):
        ref = ring_ref(n, at)
        pltpu.make_async_copy(ref, ref, ring_recv.at[n, at]).wait()

    def sib_copy(kind, at):
        buf = (abuf, abuf, zbuf)[kind]
        rows = (pl.ds(0, KB), pl.ds(KB, AR - KB), pl.ds(0, KB))[kind]
        return pltpu.make_async_remote_copy(
            src_ref=buf.at[at, rows],
            dst_ref=buf.at[at + 8, rows],
            send_sem=sib_send.at[kind, at],
            recv_sem=sib_recv.at[kind, at],
            device_id={"seq": sibling},
            device_id_type=MESH,
        )

    def k_block(at):
        m = at % 8
        rel = (m // 5) * (2 * m - 4) - m
        side = at // 8
        core = c + side - 2 * c * side
        return ((y + rel + RING) % RING) * 2 + core

    def hid_cols(at):
        return hid[:, pl.ds(pl.multiple_of(k_block(at) * KB, KB), KB)]

    def mul_t(at):
        bacc[...] += dot(abuf[at, KB:AR, :], hid_cols(at), NT)

    def mul_x(at):
        xacc[...] += dot(hid_cols(at), abuf[at, 0:KB, :])

    def mul_z(at):
        zacc[...] += dot(hid_cols(at), zbuf[at])

    muls = (mul_x, mul_t, mul_z)

    def use_mine(kind, d, count):
        def one(i, carry):
            muls[kind](d + 4 * i)
            return carry

        lax.fori_loop(0, count, one, 0)

    def use_sib(kind, d, count):
        def one(i, carry):
            sib_copy(kind, d + 4 * i).wait_recv()
            muls[kind](8 + d + 4 * i)
            return carry

        lax.fori_loop(0, count, one, 0)

    for n in (0, 1, 2):
        ring_copy(n, 0, 0).start()
        ring_copy(n, 1, 0).start()
    sib_copy(1, 0).start()
    sib_copy(0, 0).start()
    xacc[...] = jnp.zeros_like(xacc)
    zacc[...] = jnp.zeros_like(zacc)
    bacc[...] = jnp.zeros_like(bacc)

    for load in loads[6:]:
        load.wait()
    lengths = jnp.broadcast_to(len_ref[...].astype(F32), (8, SPANS))
    ends = lengths
    step = 1
    while step < SPANS:
        moved = jnp.concatenate([jnp.zeros((8, step), F32), ends[:, : SPANS - step]], axis=1)
        ends = ends + moved
        step *= 2
    starts = ends - lengths
    member = (jnp.broadcast_to(own_ref[...], (8, SPANS)) == iota((8, SPANS), 0)).astype(F32)
    before = (iota((SPANS, SPANS), 0) < iota((SPANS, SPANS), 1)).astype(F32)
    rank = dot(member, before)
    slot = iota((8, SPANS), 0).astype(F32)
    pos = (iota((8, TOK), 1) + seq * TOK).astype(F32)
    own_first = jnp.zeros((8, 1), F32)
    own_last = jnp.zeros((8, 1), F32)
    for o in range(NIVF):
        chosen = jnp.where(rank[o : o + 1, :] == slot, member[o : o + 1, :], 0.0)
        pick_slots[o * 8 : o * 8 + 8, :] = chosen
        first = jnp.sum(chosen * starts, axis=1, keepdims=True)
        last = jnp.sum(chosen * ends, axis=1, keepdims=True)
        own_first = jnp.where(ivf == o, first, own_first)
        own_last = jnp.where(ivf == o, last, own_last)
    own_ins = ((pos >= own_first) & (pos < own_last)).astype(F32).astype(BF16)
    own_inv = 1.0 / jnp.maximum(own_last - own_first, 1.0)
    span_row = iota((SPANS, SPANS), 0) == iota((SPANS, SPANS), 1)
    span_first = jnp.sum(jnp.where(span_row, starts[0:1, :], 0.0), axis=1, keepdims=True)
    span_last = jnp.sum(jnp.where(span_row, ends[0:1, :], 0.0), axis=1, keepdims=True)
    span_pos = (iota((SPANS, TOK), 1) + seq * TOK).astype(F32)
    ins[...] = ((span_pos >= span_first) & (span_pos < span_last)).astype(F32)
    span_inv = 1.0 / (span_last - span_first)

    def a2a_start(kind, src_of, dst_of):
        for k in range(n_seq):
            pltpu.make_async_remote_copy(
                src_ref=src_of(k),
                dst_ref=dst_of(k),
                send_sem=a2a_send.at[kind],
                recv_sem=a2a_recv.at[kind],
                device_id={"seq": other(k)},
                device_id_type=MESH,
            ).start()

    def a2a_wait(kind, ref):
        pltpu.make_async_copy(ref, ref, a2a_recv.at[kind]).wait()

    def a2a_sent(kind, ref):
        pltpu.make_async_copy(ref, ref, a2a_send.at[kind]).wait()

    loads[3].wait()
    loads[4].wait()
    def u_block(s, carry):
        cols = pl.ds(pl.multiple_of(s * KB + (head // 2) * 128, 128), 128)
        usrc[s] = dot(own_ins, hid[:, cols]) * own_inv
        return carry

    lax.fori_loop(0, SEQ, u_block, 0)


    def z_start(n):
        ring_copy(n, 0, 0).start()
        ring_copy(n, 1, 0).start()

    def z_step(n, d):
        ring_wait(n, d)
        if d < cuts[n][2]:
            ring_copy(n, 0, d).start()
        ring_wait(n, 4 + d)
        if d < cuts[n][3]:
            ring_copy(n, 1, d).start()
        if n == 4:
            sib_copy(2, d).start()
            sib_copy(2, 4 + d).start()

    def a_step(d, carry):
        before = 1 + (d + 1) // 3
        ring_wait(0, d)
        ring_copy(0, 0, d).start()
        ring_wait(0, 4 + d)

        @pl.when(d < 3)
        def _():
            ring_copy(0, 1, d).start()

        sib_copy(1, d).start()
        sib_copy(1, 4 + d).start()
        use_mine(1, d - 1, before)
        use_mine(0, d - 1, before)
        ring_wait(1, 4 + d)
        ring_copy(1, 1, d).start()
        ring_wait(1, d)

        @pl.when(d < 3)
        def _():
            ring_copy(1, 0, d).start()

        use_sib(1, d - 1, before)
        use_sib(0, d - 1, before)
        ring_wait(2, d)
        ring_copy(2, 0, d).start()
        ring_wait(2, 4 + d)

        @pl.when(d < 3)
        def _():
            ring_copy(2, 1, d).start()

        sib_copy(0, d).start()
        sib_copy(0, 4 + d).start()

        @pl.when(d == 3)
        def _():
            z_start(3)
            z_start(4)

        return carry

    lax.fori_loop(1, 4, a_step, 0)
    ring_wait(0, 4)
    sib_copy(1, 4).start()
    use_mine(1, 3, 2)
    use_sib(1, 3, 2)
    mul_t(4)
    use_sib(1, 4, 1)

    for part in (0, 1):
        bcbuf[part, piece] = bacc[part * HALF : part * HALF + HALF, :].astype(BF16)

    def bc_copy(part, j):
        peer = (ivf // SHARE) * SHARE + lax.rem(piece + j, SHARE)
        return pltpu.make_async_remote_copy(
            src_ref=bcbuf.at[part, piece],
            dst_ref=bcbuf.at[part, piece],
            send_sem=bc_send.at[part],
            recv_sem=bc_recv.at[part],
            device_id={"ivf": peer},
            device_id_type=MESH,
        )

    def bc_wait(part, sem):
        ref = bcbuf.at[part, pl.ds(0, SHARE - 1)]
        pltpu.make_async_copy(ref, ref, sem.at[part]).wait()

    for j in (2, 1, 3):
        bc_copy(0, j).start()

    diag = iota((8, LH), 0) == iota((8, LH), 1)
    bias = jnp.sum(jnp.where(diag, bias_ref[...], 0.0), axis=1, keepdims=True)
    rate = jnp.sum(jnp.where(diag, rate_ref[...], 0.0), axis=1, keepdims=True)
    skip = jnp.sum(jnp.where(diag, skip_ref[...], 0.0), axis=1, keepdims=True)
    raw = bacc[BCR : BCR + 8, :] + bias
    step_size = jnp.maximum(raw, 0.0) + jnp.log1p(jnp.exp(-jnp.abs(raw)))
    cum = lane_sums(-step_size * rate)
    total = cum[:, TOK - 1 : TOK]
    cumt[...] = cum
    dtt[...] = step_size
    spread = (iota((8, CH), 1) // HEAD_DIM == iota((8, CH), 0)).astype(F32)
    tail = dot(jnp.exp(total - cum) * step_size, spread, TN, HIGHEST)
    total_row = jnp.sum(total * spread, axis=0, keepdims=True)
    skip_row = jnp.sum(skip * spread, axis=0, keepdims=True)
    for half in (0, 1):
        dmsg[half] = jnp.broadcast_to(total_row[:, half * 128 : half * 128 + 128], (8, 128))
    a2a_start(3, lambda k: dmsg.at[other(k) % 2], lambda k: drecv.at[seq])
    drecv[seq] = dmsg[c]
    use_mine(0, 3, 2)
    use_sib(0, 3, 2)
    ring_wait(1, 4)
    ring_wait(2, 4)
    sib_copy(0, 4).start()
    z_step(3, 1)
    z_step(4, 1)
    sib_copy(2, 0).start()
    mul_x(4)

    use_sib(0, 4, 1)
    x_b = xacc[...].astype(BF16)
    x_f = x_b.astype(F32)
    w_hi, w_lo = split(x_f * tail)

    bc_wait(0, bc_recv)
    b_t = bcbuf[0].reshape(STATE, TOK)
    end_state = dot(b_t, w_hi) + dot(b_t, w_lo)
    for s in range(SEQ):
        r, half = s // 2, s % 2
        cols = slice(half * 128, half * 128 + 128)
        smsg[s] = end_state[r * 16 : r * 16 + 16, cols]
    a2a_start(1, lambda k: smsg.at[other(k)], lambda k: srecv.at[seq])
    srecv[seq] = smsg[seq]

    for j in (2, 1, 3):
        bc_copy(1, j).start()
    z_step(3, 2)
    z_step(4, 2)
    bc_wait(1, bc_recv)
    c_m = bcbuf[1].reshape(STATE, TOK).astype(F32).T.astype(BF16)
    scores[...] = dot(c_m, b_t)
    ybuf[...] = x_f * skip_row
    ecum[...] = dot(jnp.exp(cum), spread, TN, HIGHEST)

    def one_head(h, carry):
        pick = (iota((8, 128), 0) == h).astype(F32)
        rep = dot(cumt[...], pick, TN, HIGHEST)
        xm = jnp.where(iota((TOK, CH), 1) // HEAD_DIM == h, x_f, 0.0).astype(BF16)
        cum_row = cumt[pl.ds(h, 1), :]
        dt_row = dtt[pl.ds(h, 1), :]
        for i in range(4):
            parts = []
            here = slice(i * 128, i * 128 + 128)
            for k in range(i + 1):
                cols = slice(k * 128, k * 128 + 128)
                between = rep[here, :] - cum_row[:, cols]
                if k == i:
                    between = jnp.where(iota((128, 128), 0) >= iota((128, 128), 1), between, -1e30)
                weight = scores[here, cols] * jnp.exp(between) * dt_row[:, cols]
                parts.append(weight.astype(BF16))
            block = jnp.concatenate(parts, axis=1) if i else parts[0]
            ybuf[here, :] += dot(block, xm[0 : i * 128 + 128, :])
        return carry

    lax.fori_loop(0, LH, one_head, 0)
    a2a_wait(3, drecv.at[pl.ds(0, n_seq)])
    a2a_wait(1, srecv.at[pl.ds(0, n_seq)])

    def enter(s, carried):
        sout[s] = carried
        return jnp.exp(drecv[s][0:1, :]) * carried + srecv[s]

    lax.fori_loop(0, SEQ, enter, jnp.zeros((16, 128), F32))
    a2a_start(2, lambda k: sout.at[other(k)], lambda k: sin.at[seq])
    sin[seq] = sout[seq]
    z_step(3, 3)
    z_step(4, 3)
    mul_z(0)
    use_sib(2, 0, 1)
    use_mine(2, 1, 2)
    use_sib(2, 1, 2)

    use_mine(2, 2, 2)
    use_sib(2, 2, 2)
    loads[5].wait()
    at_col = iota((CH, NHEAD * 128), 1)
    wanted = (at_col // 128) * 64 + at_col % 128
    take = (at_col % 128 < 64) & (wanted == iota((CH, NHEAD * 128), 0))
    wpad[...] = dot(wout[...], take.astype(F32).astype(BF16)).astype(BF16)
    ring_wait(3, 4)
    ring_wait(4, 4)
    sib_copy(2, 4).start()
    use_mine(2, 3, 2)
    use_sib(2, 3, 2)
    mul_z(4)
    use_sib(2, 4, 1)
    z = zacc[...].astype(BF16).astype(F32)
    gate = z / (1.0 + jnp.exp(-z))

    a2a_start(0, lambda k: usrc.at[other(k)], lambda k: urecv.at[k])
    a2a_wait(2, sin.at[pl.ds(0, n_seq)])
    entering = jnp.concatenate(
        [jnp.concatenate([sin[2 * r], sin[2 * r + 1]], axis=1) for r in range(8)], axis=0
    )
    e_hi, e_lo = split(entering)
    gated = (ybuf[...] + ecum[...] * (dot(c_m, e_hi) + dot(c_m, e_lo))) * gate
    square = (gated * gated).astype(BF16)
    same = (iota((CH, CH), 0) // HEAD_DIM == iota((CH, CH), 1) // HEAD_DIM).astype(F32).astype(BF16)
    mean_sq = dot(square, same) * (1.0 / HEAD_DIM)
    normed = (gated * lax.rsqrt(mean_sq + 1e-05) * gain_ref[...]).astype(BF16)
    pooled = dot(ins[...].astype(BF16), normed) * span_inv
    psrc[0] = pooled[:, 0:128]
    psrc[1] = pooled[:, 128:256]

    def to_sibling(kind, src, dst):
        return pltpu.make_async_remote_copy(
            src_ref=src,
            dst_ref=dst,
            send_sem=p_send.at[kind],
            recv_sem=p_recv.at[kind],
            device_id={"seq": sibling},
            device_id_type=MESH,
        )

    first_half = to_sibling(0, psrc.at[1 - c], psib)
    first_half.start()
    first_half.wait_recv()
    pall[y] = (psrc[c] + psib[...]).astype(BF16)

    for k in range(RING - 1):
        peer = lax.rem(y + outward(k, RING // 2), RING) * 2 + c
        pltpu.make_async_remote_copy(
            src_ref=pall.at[y],
            dst_ref=pall.at[y],
            send_sem=p_send.at[1],
            recv_sem=p_recv.at[1],
            device_id={"seq": peer},
            device_id_type=MESH,
        ).start()

    most = pall.at[pl.ds(0, RING - 1)]
    pltpu.make_async_copy(most, most, p_recv.at[1]).wait()
    phalf[c] = jnp.sum(pall[...].astype(F32), axis=0)
    second_half = to_sibling(2, phalf.at[c], phalf.at[c])
    second_half.start()
    second_half.wait_recv()
    s_hi, s_lo = split(jnp.concatenate([phalf[0], phalf[1]], axis=1))
    slots = pick_slots[...].astype(BF16)
    value = dot(dot(slots, s_hi).astype(BF16), wpad[...]) + dot(
        dot(slots, s_lo).astype(BF16), wpad[...]
    )
    for o in range(NIVF):
        for h in range(NHEAD):
            fsrc[h * NIVF + o] = value[o * 8 : o * 8 + 8, h * 128 : h * 128 + 128]

    for k in range(n_far):
        h, o = far(k)
        pltpu.make_async_remote_copy(
            src_ref=fsrc.at[h * NIVF + o],
            dst_ref=frecv.at[k],
            send_sem=f_send,
            recv_sem=f_recv,
            device_id={"head": h, "ivf": o},
            device_id_type=MESH,
        ).start()

    def sent(d, carry):
        for n in range(5):
            for direction in (0, 1):
                if cuts[n][2 + direction] == 4:
                    ring_copy(n, direction, d).wait_send()
                else:

                    @pl.when(d < 3)
                    def _():
                        ring_copy(n, direction, d).wait_send()

        return carry

    def sib_sent(at, carry):
        for kind in range(3):
            sib_copy(kind, at).wait_send()
        return carry

    lax.fori_loop(0, 4, sent, 0)
    lax.fori_loop(0, 8, sib_sent, 0)
    bc_wait(0, bc_send)
    bc_wait(1, bc_send)
    a2a_sent(0, urecv)
    a2a_sent(1, srecv.at[pl.ds(0, n_seq)])
    a2a_sent(2, sin.at[pl.ds(0, n_seq)])
    a2a_sent(3, drecv.at[pl.ds(0, n_seq)])
    first_half.wait_send()
    second_half.wait_send()
    pltpu.make_async_copy(most, most, p_send.at[1]).wait()

    a2a_wait(0, urecv)
    mean_u = usrc[seq] + jnp.sum(urecv[...], axis=0)
    mean_u = jnp.where(head % 2 == 0, mean_u[:, 0:64], mean_u[:, 64:128])
    own = fsrc[head * NIVF + ivf]
    pltpu.make_async_copy(frecv, frecv, f_recv).wait()
    result = (own + jnp.sum(frecv[...], axis=0))[:, 0:64] + mean_u
    out_ref[:, 0, :] = result[0:CAP, :]
    pltpu.make_async_copy(frecv, frecv, f_send).wait()


def local(
    hidden_in, w_x, w_z, w_dt, w_bc, dt_bias, a_rate, d_skip, norm_gain, w_out, span_lengths, owners
):
    any_spec = pl.BlockSpec(memory_space=pl.ANY)
    vmem_spec = pl.BlockSpec(memory_space=pltpu.VMEM)
    vmem = pltpu.VMEM
    dma = pltpu.SemaphoreType.DMA
    rows = pl.pallas_call(
        kernel,
        out_shape=jax.ShapeDtypeStruct((CAP, 1, 64), F32),
        in_specs=[any_spec] * 12,
        out_specs=vmem_spec,
        scratch_shapes=[
            vmem((1, SPANS), jnp.int32),
            vmem((1, SPANS), jnp.int32),
            vmem((1, LH), F32),
            vmem((1, LH), F32),
            vmem((1, LH), F32),
            vmem((1, CH), F32),
            vmem((TOK, SEQ * KB), BF16),
            vmem((SEQ, AR, CH), BF16),
            vmem((SEQ, KB, CH), BF16),
            vmem((TOK, CH), F32),
            vmem((TOK, CH), F32),
            vmem((BCR + DTR, TOK), F32),
            vmem((2, SHARE, HALF, TOK), BF16),
            vmem((KB, 2 * STATE), BF16),
            vmem((LH, KB), BF16),
            vmem((CH, 256), BF16),
            vmem((CH, NHEAD * 128), BF16),
            vmem((64, SPANS), F32),
            vmem((SPANS, TOK), F32),
            vmem((SEQ, 8, 128), F32),
            vmem((SEQ - 1, 8, 128), F32),
            vmem((2, 8, 128), F32),
            vmem((SEQ, 8, 128), F32),
            vmem((SEQ, 16, 128), F32),
            vmem((SEQ, 16, 128), F32),
            vmem((SEQ, 16, 128), F32),
            vmem((SEQ, 16, 128), F32),
            vmem((TOK, TOK), F32),
            vmem((8, TOK), F32),
            vmem((8, TOK), F32),
            vmem((TOK, CH), F32),
            vmem((TOK, CH), F32),
            vmem((2, SPANS, 128), F32),
            vmem((SPANS, 128), F32),
            vmem((RING, SPANS, 128), BF16),
            vmem((2, SPANS, 128), F32),
            vmem((NHEAD * NIVF, 8, 128), F32),
            vmem((NHEAD * NIVF - 1, 8, 128), F32),
            dma((12,)),
            dma((5, 2, 4)),
            dma((5, 8)),
            dma((3, 8)),
            dma((3, 8)),
            dma((2,)),
            dma((2,)),
            dma((4,)),
            dma((4,)),
            dma((3,)),
            dma((3,)),
            dma,
            dma,
        ],
        compiler_params=pltpu.CompilerParams(
            collective_id=0, has_side_effects=True, vmem_limit_bytes=64 * 1024 * 1024
        ),
    )(
        hidden_in,
        w_x,
        w_z,
        w_dt.T,
        w_bc,
        w_out,
        span_lengths.reshape(1, SPANS),
        owners.T,
        dt_bias.reshape(1, LH),
        a_rate.reshape(1, LH),
        d_skip.reshape(1, LH),
        norm_gain.reshape(1, CH),
    )
    return jnp.transpose(rows, (1, 0, 2))


def solution(mesh):
    return jax.shard_map(
        local,
        mesh=mesh,
        in_specs=(
            P("seq", None),
            P("seq", ("head", "ivf")),
            P("seq", ("head", "ivf")),
            P("seq", ("head", "ivf")),
            P("seq", "head"),
            P(("head", "ivf")),
            P(("head", "ivf")),
            P(("head", "ivf")),
            P(("head", "ivf")),
            P(("head", "ivf"), "seq"),
            P(),
            P(),
        ),
        out_specs=P("ivf", None, ("seq", "head")),
        check_vma=False,
    )
```
